128 devices in a mesh: expert: 4 (over x), zero: 32 (over z, y, core).
Axes of the slice: x: 4, y: 4, z: 4, core: 2. Of those that a mesh axis runs over, the one named last changes fastest.
Arguments:
- tokens: bfloat16 [16384, 1024], P(('expert', 'zero')), may hold values from -6 to 6
- grads_out: bfloat16 [16384, 1024], P(('expert', 'zero')), may hold values from -1.1953125 to 1.1953125
- routes: int32 [16384, 2], P(('expert', 'zero')), may hold values from 0 to 3, as said below
- slots: int32 [16384, 2], P(('expert', 'zero')), may hold values from 0 to 64, as said below
- combine: bfloat16 [16384, 2], P(('expert', 'zero')), may hold values from 0.049804688 to 1
- w_in: bfloat16 [4, 1024, 4096], P('expert', None, 'zero'), may hold values from -0.1875 to 0.1875
- b_in: bfloat16 [4, 4096], P('expert', 'zero'), may hold values from -3 to 3
- w_out: bfloat16 [4, 4096, 1024], P('expert', 'zero'), may hold values from -0.09375 to 0.09375
- b_out: bfloat16 [4, 1024], P('expert'), may hold values from -0.59765625 to 0.59765625
Outputs:
- grad_tokens: bfloat16 [16384, 1024], P(('expert', 'zero'))
- grad_combine: float32 [16384, 2], P(('expert', 'zero'))
- grad_w_in: bfloat16 [4, 1024, 4096], P('expert', None, 'zero')
- grad_b_in: float32 [4, 4096], P('expert', 'zero')
- grad_w_out: bfloat16 [4, 4096, 1024], P('expert', 'zero')
- grad_b_out: float32 [4, 1024], P('expert')
The draws below stay inside these ranges and needn't reach their ends.
Inputs may be any that keep to these rules, and one draw needn't show every extreme that they name: `routes`: each row names 2 different experts. Within the rows of one device (aligned blocks of 128 rows), the choices that name one expert, taken in order of row and then of column, hold the slots 0, 1, 2 and so on; once 64 of them are taken, every further such choice holds 64 and is dropped.
All inputs are finite; a program needn't handle non-finite values.
Results may differ from the reference program's by a relative error of at most 0.0065.
Values may be sent and summed in bfloat16 or wider, within the bound.
No kernel may reach another device: no remote copies, remote signals or barrier semaphores. Data moves between devices by JAX's collectives and lax.ppermute only.
A program may use at most 128 MiB of HBM per device.

```python
import jax
import jax.numpy as jnp
from jax import lax

D = 1024
FF = 4096
TOK_DEV = 128
TOP = 2
EXPERT_COUNT = 4
CAP = 64
TOKENS = 16384
N_EXPERT = 4
N_ZERO = 32


def assignments(key):
    blocks = TOKENS // TOK_DEV
    key_hot, key_pop, key_base, key_perm = jax.random.split(key, 4)
    hot_expert = jax.random.randint(key_hot, (), 0, EXPERT_COUNT)
    popular_expert = jax.random.randint(key_pop, (EXPERT_COUNT,), 0, 4)
    baseline_score = jax.random.randint(key_base, (TOKENS, EXPERT_COUNT), 0, 4096)

    def shuffle(one_key):
        return jax.random.permutation(one_key, TOK_DEV)
    ranks = jax.vmap(shuffle)(jax.random.split(key_perm, blocks))
    forced_expert = (ranks <= CAP).reshape(TOKENS)
    expert_positions = jnp.arange(EXPERT_COUNT, dtype=jnp.int32)
    extra_score = jnp.where(forced_expert[:, None] & (expert_positions[None, :] == hot_expert), 100000, 0)
    routing_score = (baseline_score + popular_expert[None, :] * 2048 + extra_score) * EXPERT_COUNT + expert_positions[None, :]
    _, chosen = lax.top_k(routing_score, TOP)
    chosen = chosen.astype(jnp.int32)
    named = (chosen.reshape(blocks, TOK_DEV * TOP)[:, :, None] == expert_positions[None, None, :]).astype(jnp.int32)
    before = jnp.cumsum(named, axis=1) - named
    position = jnp.sum(before * named, axis=2)
    position = jnp.minimum(position, CAP).reshape(TOKENS, TOP).astype(jnp.int32)
    return (chosen, position)


def draw_routes(key, part):
    chosen, position = assignments(key)
    return chosen


def draw_slots(key, part):
    chosen, position = assignments(key)
    return position


def levels(rng, dims, shards, low, top_value):
    level, own = 1.0, jax.random.fold_in(rng, 6)
    for dim, shards_of in shards:
        heights = jnp.exp(jax.random.uniform(jax.random.fold_in(own, dim), (shards_of,), jnp.float32, low / len(shards), top_value / len(shards)))
        level = level * jnp.repeat(heights, dims[dim] // shards_of).reshape([-1 if axis == dim else 1 for axis in range(len(dims))])
    return level


def scatter_about(key, dims, deviation, bound, cuts=(), kind=jnp.bfloat16):
    values = deviation * jax.random.normal(key, dims, jnp.float32)
    if cuts:
        values = values * levels(key, dims, cuts, -0.22, 0.18)
    return jnp.clip(values, -bound, bound).astype(kind)


def setup_inputs(seed: int = 0) -> dict:
    splits = jax.random.split(jax.random.key(seed), 10)
    return {
        "tokens": scatter_about(splits[0], (TOKENS, D), 1.0, 6.0, ((0, 128),)),
        "grads_out": scatter_about(splits[1], (TOKENS, D), 0.2, 1.1953125, ((0, 128),)),
        "routes": draw_routes(jax.random.fold_in(splits[9], 71), 0),
        "slots": draw_slots(jax.random.fold_in(splits[9], 71), 0),
        "combine": jnp.clip(0.049804688 + 0.9501953 * jax.random.uniform(splits[4], (TOKENS, TOP), jnp.float32) ** levels(splits[4], (TOKENS, TOP), ((0, 128),), -0.2, 0.2), 0.049804688, 1.0).astype(jnp.bfloat16),
        "w_in": scatter_about(splits[5], (EXPERT_COUNT, D, FF), D ** -0.5, 0.1875, ((0, 4), (2, 32))),
        "b_in": scatter_about(splits[6], (EXPERT_COUNT, FF), 0.5, 3.0, ((0, 4), (1, 32))),
        "w_out": scatter_about(splits[7], (EXPERT_COUNT, FF, D), FF ** -0.5, 0.09375, ((0, 4), (1, 32))),
        "b_out": scatter_about(splits[8], (EXPERT_COUNT, D), 0.1, 0.59765625, ((0, 4),)),
    }


def gelu_parts(pre):
    cdf = 0.5 * (1.0 + lax.erf(pre * 0.7071067811865476))
    dens = jnp.exp(-0.5 * pre * pre) * 0.3989422804014327
    return pre * cdf, cdf + pre * dens


def grouped_sum(left, right):
    left_g = left.reshape(N_EXPERT, N_ZERO, CAP, -1).transpose(1, 0, 2, 3).reshape(N_ZERO, N_EXPERT * CAP, -1)
    right_g = right.reshape(N_EXPERT, N_ZERO, CAP, -1).transpose(1, 0, 2, 3).reshape(N_ZERO, N_EXPERT * CAP, -1)

    def add_group(total, pair):
        part = jnp.dot(pair[0].T, pair[1], preferred_element_type=jnp.float32).astype(jnp.bfloat16)
        part = lax.optimization_barrier(part)
        return total + part.astype(jnp.float32), None

    start = jnp.zeros((left.shape[1], right.shape[1]), jnp.float32)
    total, _ = lax.scan(add_group, start, (left_g, right_g))
    return total.astype(jnp.bfloat16)


def expert_backward(items):
    w_in, b_in, w_out, b_out, rows_x, rows_g, rows_c = items
    pre = jnp.dot(rows_x, w_in, preferred_element_type=jnp.float32) + b_in.astype(jnp.float32)[None, :]
    hidden32, slope = gelu_parts(pre)
    hidden = hidden32.astype(jnp.bfloat16)
    back = jnp.dot(rows_g, w_out.T, preferred_element_type=jnp.float32)
    weight = rows_c.astype(jnp.float32)[:, None]
    dcomb = jnp.sum(hidden32 * back, axis=1) + jnp.sum(rows_g.astype(jnp.float32) * b_out.astype(jnp.float32)[None, :], axis=1)
    dout = (weight * rows_g.astype(jnp.float32)).astype(jnp.bfloat16)
    dpre = (weight * back * slope).astype(jnp.bfloat16)
    grad_in = grouped_sum(rows_x, dpre)
    grad_bias_in = jnp.sum(dpre.astype(jnp.float32), axis=0)
    grad_out = grouped_sum(hidden, dout)
    grad_bias_out = jnp.sum(dout.astype(jnp.float32), axis=0)
    slot_dx = jnp.dot(dpre, w_in.T, preferred_element_type=jnp.float32)
    return grad_in, grad_bias_in, grad_out, grad_bias_out, slot_dx, dcomb


def reference(tokens, grads_out, routes, slots, combine, w_in, b_in, w_out, b_out):
    blocks = TOKENS // TOK_DEV
    depth = blocks * CAP
    block_of = (jnp.arange(TOKENS, dtype=jnp.int32) // TOK_DEV).astype(jnp.int32)
    kept = slots < CAP
    places = jnp.where(kept, block_of[:, None] * CAP + slots, depth).astype(jnp.int32)
    flat_e = routes.reshape(-1).astype(jnp.int32)
    flat_p = places.reshape(-1).astype(jnp.int32)
    rep_x = jnp.repeat(tokens, TOP, axis=0)
    rep_g = jnp.repeat(grads_out, TOP, axis=0)
    buf_x = jnp.zeros((EXPERT_COUNT, depth, D), tokens.dtype).at[flat_e, flat_p].set(rep_x, mode="drop")
    buf_g = jnp.zeros((EXPERT_COUNT, depth, D), grads_out.dtype).at[flat_e, flat_p].set(rep_g, mode="drop")
    buf_c = jnp.zeros((EXPERT_COUNT, depth), combine.dtype).at[flat_e, flat_p].set(combine.reshape(-1), mode="drop")
    grad_w_in, grad_b_in, grad_w_out, grad_b_out, slot_dx, slot_dc = lax.map(
        expert_backward, (w_in, b_in, w_out, b_out, buf_x, buf_g, buf_c))
    safe_p = jnp.where(kept, places, 0).astype(jnp.int32)
    keep32 = kept.astype(jnp.float32)
    picked_dx = slot_dx[routes, safe_p] * keep32[:, :, None]
    grad_tokens = jnp.sum(picked_dx, axis=1).astype(jnp.bfloat16)
    grad_combine = slot_dc[routes, safe_p] * keep32
    return grad_tokens, grad_combine, grad_w_in, grad_b_in, grad_w_out, grad_b_out
```

```python
import functools

import jax
import jax.numpy as jnp
from jax import lax
from jax.experimental import pallas as pl
from jax.experimental.pallas import tpu as pltpu
from jax.sharding import Mesh, PartitionSpec as P

BF = jnp.bfloat16
F32 = jnp.float32
EXTRA = 16
NT = (((1,), (1,)), ((), ()))
NN = (((1,), (0,)), ((), ()))
TN = (((0,), (0,)), ((), ()))


def dot(a, b, dims):
    return lax.dot_general(a, b, dims, preferred_element_type=F32)


def shift(value, axis, step):
    n = lax.axis_size(axis)
    return lax.ppermute(value, axis, [(i, (i + step) % n) for i in range(n)])


def call(kernel, name, out_shape, flops=0, bytes_accessed=0, **options):
    return pl.pallas_call(
        kernel,
        out_shape=out_shape,
        compiler_params=pltpu.CompilerParams(vmem_limit_bytes=48 * 1024 * 1024),
        cost_estimate=pl.CostEstimate(
            flops=flops, bytes_accessed=bytes_accessed, transcendentals=0
        ),
        name=name,
        **options,
    )


def shape(rows, columns, dtype=BF):
    return jax.ShapeDtypeStruct((rows, columns), dtype)


def high_low(value):
    high = value.astype(BF).astype(F32)
    return high, value - high


def pack_kernel(places, weights, tokens, grads, *outs):
    slots = outs[0].shape[1]
    spots = lax.broadcasted_iota(jnp.int32, (len(outs) * slots, tokens.shape[0]), 0)
    first = places[0:1, :] == spots
    second = places[1:2, :] == spots
    picks = jnp.where(first | second, 1.0, 0.0).astype(BF)
    scaled = (
        jnp.where(first, weights[0:1, :], 0.0) + jnp.where(second, weights[1:2, :], 0.0)
    ).astype(BF)
    rows_x = dot(picks, tokens[...], NN).astype(BF)
    rows_d = dot(scaled, grads[...], NN).astype(BF)
    for s, out in enumerate(outs):
        out[0] = rows_x[s * slots : (s + 1) * slots]
        out[1] = rows_d[s * slots : (s + 1) * slots]


def rows_kernel(counts, lead, n_w, block, *refs):
    n_parts = len(counts)
    n_z = 4
    refs = list(refs)
    parts_x = [[refs.pop(0) for _ in range(n_parts)] for _ in range(n_z)]
    parts_d = [[refs.pop(0) for _ in range(n_parts)] for _ in range(n_z)]
    w = [refs.pop(0) for _ in range(n_w)]
    b_out = refs.pop(0)
    x, d, dpre, hidden, *dxs = refs[: 4 + n_z]
    acc, prod = refs[4 + n_z :]
    m = sum(counts)
    width = x.shape[1]
    for z in range(n_z):
        at = z * m
        for p, count in enumerate(counts):
            x[at : at + count] = parts_x[z][p][...].reshape(count, width)
            d[at : at + count] = parts_d[z][p][...].reshape(count, width)
            at += count
    unit = 128
    tiles = []
    for k in range(4):
        if k < 3:
            ours, other = w[2 * k], w[2 * k + 1]
            halves = [(r[0:unit], r[unit : unit + 1], r[unit + EXTRA :]) for r in (ours, other)]
        else:
            halves = [
                (r[0:unit], r[unit : unit + 1], s[...]) for r, s in ((w[6], w[7]), (w[8], w[9]))
            ]
        tiles.append(halves)

    def body(i, _):
        rows = pl.ds(pl.multiple_of(i * block, block), block)
        xb = x[rows]
        db = d[rows]
        total = None
        term = None
        for k, halves in enumerate(tiles):
            w_in = jnp.concatenate([h[0] for h in halves], axis=0)
            bias = jnp.concatenate([h[1][:, 0:unit] for h in halves], axis=1).astype(F32)
            w_out = jnp.concatenate([h[2] for h in halves], axis=0)
            pre = dot(xb, w_in, NT) + bias
            back = dot(db, w_out, NT)
            cdf = 0.5 * (1.0 + lax.erf(pre * 0.7071067811865476))
            dens = jnp.exp(-0.5 * pre * pre) * 0.3989422804014327
            hidden32 = pre * cdf
            grad = (back * (cdf + pre * dens)).astype(BF)
            hid = hidden32.astype(BF)
            for c in range(2):
                columns = slice((4 * c + k) * unit, (4 * c + k + 1) * unit)
                dpre[rows, columns] = grad[:, c * unit : (c + 1) * unit]
                hidden[rows, columns] = hid[:, c * unit : (c + 1) * unit]
            new = hidden32 * back
            part = dot(grad, w_in, NN)
            total = part if k == 0 else total + part
            term = new if k == 0 else term + new
        acc[rows] = total
        prod[i] = jnp.broadcast_to(jnp.sum(term.T, axis=0, keepdims=True), prod.shape[1:])
        return 0

    n_blocks = n_z * m // block
    lax.fori_loop(0, n_blocks, body, 0)
    by_bias = jnp.sum((d[0:m].astype(F32) * b_out[...].astype(F32)).T, axis=0, keepdims=True)
    for z in range(n_z):
        out = dxs[z]
        out[0:m] = acc[z * m : (z + 1) * m].astype(out.dtype)
        if block == m:
            line = prod[z][0:1, 0:m]
        else:
            line = prod[0][0:1, z * m : (z + 1) * m]
        if z == 0:
            line = line + by_bias
        if out.dtype == F32:
            lines = [line, jnp.zeros_like(line)]
        else:
            lines = list(high_low(line))
        sums = jnp.concatenate(lines + [jnp.zeros((EXTRA - 2, m), F32)], axis=0)
        out[m:] = jnp.zeros((EXTRA, width), out.dtype)
        out[m:, 0:m] = sums.astype(out.dtype)


def rows_set(parts_x, parts_d, w, b_out, block):
    counts = [a.shape[1] for a, _ in parts_x[0]]
    m = sum(counts)
    width = b_out.shape[1]
    units = 1024

    def piece(pair):
        array, index = pair
        return pl.BlockSpec((1, *array.shape[1:]), lambda i, index=index: (index, 0, 0))

    def full(a):
        return pl.BlockSpec(a.shape, lambda i: (0,) * len(a.shape))

    pieces = [pair for z in parts_x for pair in z] + [pair for z in parts_d for pair in z]
    out_shape = [shape(4 * m, width), shape(4 * m, width), shape(4 * m, units), shape(4 * m, units)]
    out_shape += [shape(m + EXTRA, width, F32 if z == 0 else BF) for z in range(4)]
    return call(
        functools.partial(rows_kernel, counts, None, len(w), block),
        "rows",
        out_shape,
        flops=24 * m * units * width,
        bytes_accessed=4 * units * width + 32 * m * width,
        grid=(1,),
        in_specs=[piece(p) for p in pieces] + [full(a) for a in w] + [full(b_out)],
        out_specs=[full(s) for s in out_shape],
        scratch_shapes=[
            pltpu.VMEM((4 * m, width), F32),
            pltpu.VMEM((4 * m // block, 8, block), F32),
        ],
    )(*[a for a, _ in pieces], *w, b_out)


def weights_kernel(n_sets, with_add, *refs):
    xs, ds, dpres, hiddens = (refs[k * n_sets : (k + 1) * n_sets] for k in range(4))
    rest = refs[4 * n_sets :]
    adds, outs = (rest[:4], rest[4:]) if with_add else ((), rest)
    unit = dpres[0].shape[1] // 4
    total_in = sum(dot(p[...], x[...], TN) for p, x in zip(dpres, xs))
    total_out = sum(dot(h[...], d[...], TN) for h, d in zip(hiddens, ds))
    sum_in = sum(jnp.sum(p[...].astype(F32), axis=0, keepdims=True) for p in dpres)
    sum_out = sum(jnp.sum(d[...].astype(F32), axis=0, keepdims=True) for d in ds)
    width = total_in.shape[1]
    for k, out in enumerate(outs):
        grad_in = total_in[k * unit : (k + 1) * unit]
        grad_out = total_out[k * unit : (k + 1) * unit]
        line_in = sum_in[:, k * unit : (k + 1) * unit]
        line_out = sum_out
        if with_add:
            a = adds[k]
            grad_in = grad_in + a[0:unit].astype(F32)
            grad_out = grad_out + a[unit : 2 * unit].astype(F32)
            tail = a[2 * unit :].astype(F32)
            line_in = line_in + tail[0:1, 0:unit] + tail[1:2, 0:unit]
            line_out = line_out + tail[2:3] + tail[3:4]
        line_in = jnp.concatenate([line_in, jnp.zeros((1, width - unit), F32)], axis=1)
        lines = [line_in, line_out]
        if out.dtype == F32:
            lines = [line_in, jnp.zeros_like(line_in), line_out, jnp.zeros_like(line_out)]
        else:
            lines = [*high_low(line_in), *high_low(line_out)]
        out[0:unit] = grad_in.astype(out.dtype)
        out[unit : 2 * unit] = grad_out.astype(out.dtype)
        lines.append(jnp.zeros((EXTRA - 4, width), F32))
        out[2 * unit :] = jnp.concatenate(lines, axis=0).astype(out.dtype)


def weights_part(sets, other_core, adds):
    (x, d, dpre, hidden) = zip(*sets)
    units = dpre[0].shape[1] // 2
    width = x[0].shape[1]
    rows = sum(a.shape[0] for a in x)

    def full(a):
        return pl.BlockSpec(a.shape, lambda i: (0,) * len(a.shape))

    def cut(a):
        return pl.BlockSpec((a.shape[0], units), lambda i: (0, int(other_core)))

    height = 2 * units // 4 + EXTRA
    out_shape = [shape(height, width, F32 if adds and k == 0 else BF) for k in range(4)]
    return call(
        functools.partial(weights_kernel, len(sets), bool(adds)),
        "weights",
        out_shape,
        flops=4 * rows * units * width,
        bytes_accessed=4 * rows * width + 4 * rows * units + 4 * units * width,
        grid=(1,),
        in_specs=[full(a) for a in x + d]
        + [cut(a) for a in dpre + hidden]
        + [full(a) for a in adds],
        out_specs=[full(s) for s in out_shape],
    )(*x, *d, *dpre, *hidden, *adds)


def sum_kernel(n_out, own, *refs):
    parts, outs = refs[:-n_out], refs[-n_out:]
    m = own.shape[0] - EXTRA
    total = own[...]
    for p in parts:
        total = total + p[...].astype(F32)
    line = total[m : m + 1] + total[m + 1 : m + 2]
    lines = jnp.concatenate(
        [*high_low(line), jnp.zeros((EXTRA - 2, own.shape[1]), F32)], axis=0
    ).astype(BF)
    slots = m // n_out
    for s, out in enumerate(outs):
        out[0:slots] = total[s * slots : (s + 1) * slots].astype(BF)
        out[slots:] = lines


def sum_z(own, parts, n_out):
    slots = (own.shape[0] - EXTRA) // n_out
    return call(
        functools.partial(sum_kernel, n_out),
        "sum_z",
        [shape(slots + EXTRA, own.shape[1])] * n_out,
        bytes_accessed=12 * own.size,
    )(own, *parts)


def finish_kernel(offsets, places, weights, *refs):
    pieces, (out, by_weight) = refs[:-2], refs[-2:]
    slots = pieces[0].shape[0] - EXTRA
    n_tok = places.shape[1]
    total = None
    sums = [None, None]
    for s, piece in enumerate(pieces):
        spots = lax.broadcasted_iota(jnp.int32, (slots, n_tok), 0) + s * slots
        picks = jnp.where((places[0:1, :] == spots) | (places[1:2, :] == spots), 1.0, 0.0)
        part = dot(picks.astype(BF), piece[0:slots], TN)
        total = part if total is None else total + part
        span = lax.broadcasted_iota(jnp.int32, (256, n_tok), 0) - offsets[s]
        inside = (span >= 0) & (span < slots)
        for k in range(2):
            pick = jnp.where(inside & (places[k : k + 1, :] == span + s * slots), 1.0, 0.0)
            found = dot(piece[slots:, 0:256], pick.astype(BF), NN)
            line = found[0:1] + found[1:2]
            sums[k] = line if sums[k] is None else sums[k] + line
    out[...] = total.astype(BF)
    by_weight[...] = jnp.concatenate(sums, axis=0) / weights[...]


def on_device(tokens, grads_out, routes, slots, combine, w_in, b_in, w_out, b_out):
    n_expert = lax.axis_size("x")
    tok_rows, width = tokens.shape
    cap = 2 * tok_rows // n_expert
    me = lax.axis_index("x")

    turned = lax.rem(routes - me + n_expert, n_expert)
    places = jnp.where(slots < cap, turned * cap + slots, -1).T
    scales = combine.T.astype(F32)
    sent = call(pack_kernel, "pack", [jax.ShapeDtypeStruct((2, cap, width), BF)] * n_expert)(
        places, scales, tokens, grads_out
    )
    got_left = shift(sent[1], "x", 1)
    got_right = shift(sent[3], "x", -1)
    got_far = shift(sent[2], "x", 2)

    def along_z(part):
        below = shift(part, "z", 1)
        above = shift(part, "z", -1)
        far_x = shift(below[0:1], "z", 1)
        far_d = shift(above[1:2], "z", -1)
        x = [(part, 0), (below, 0), (above, 0), (far_x, 0)]
        d = [(part, 1), (below, 1), (above, 1), (far_d, 0)]
        return x, d

    x_a, d_a = along_z(sent[0])
    x_b, d_b = along_z(jnp.concatenate([got_left, got_right], axis=1))
    x_c, d_c = along_z(got_far)

    units = w_in.shape[2]
    bias_rows = jnp.pad(b_in, ((0, EXTRA - 1), (0, width - units)))
    mine = jnp.concatenate([w_in[0].T, bias_rows, w_out[0]], axis=0)
    below = shift(mine, "y", 1)
    above = shift(mine, "y", -1)
    cut = units + EXTRA
    far_in = shift(below[:cut], "y", 1)
    far_out = shift(above[cut:], "y", -1)
    w = []
    for a in (mine, below, above):
        w += [a, shift(a, "c", 1)]
    w += [far_in, far_out, shift(far_in, "c", 1), shift(far_out, "c", 1)]

    ab = rows_set(
        [[p, q] for p, q in zip(x_a, x_b)], [[p, q] for p, q in zip(d_a, d_b)], w, b_out, 3 * cap
    )
    c = rows_set([[p] for p in x_c], [[p] for p in d_c], w, b_out, 4 * cap)
    ways = [0, -1, 1, 2]
    pieces = {}
    for key, res, names in (("ab", ab, (0, 1, 3)), ("c", c, (2,))):
        dx = res[4:]
        moved = [shift(dx[k], "z", ways[k]) for k in (3, 1, 2)]
        for s, piece in zip(names, sum_z(dx[0], moved, len(names))):
            pieces[s] = piece

    sets = [ab[:4], c[:4]]
    away = weights_part(sets, True, ())
    home = weights_part(sets, False, [shift(a, "c", 1) for a in away])
    moved = [shift(home[k], "y", ways[k]) for k in (3, 1, 2)]
    total = home[0] + sum(a.astype(F32) for a in moved)
    grad_w_in = total[:units].T.astype(BF)[None]
    grad_w_out = total[units : 2 * units].astype(BF)[None]
    tail = total[2 * units :]
    grad_b_in = (tail[0] + tail[1])[:units][None]
    grad_b_out = (tail[2] + tail[3])[None]

    back = {0: 0, 1: -1, 2: 2, 3: 1}
    final = [shift(pieces[s], "x", back[s]) if s else pieces[s] for s in range(n_expert)]
    grad_tokens, by_weight = call(
        functools.partial(finish_kernel, (0, cap, 0, 2 * cap)),
        "finish",
        [shape(tok_rows, width), shape(2, tok_rows, F32)],
    )(places, scales, *final)
    return (grad_tokens, by_weight.T, grad_w_in, grad_b_in, grad_w_out, grad_b_out)


def solution(mesh):
    fine = Mesh(mesh.devices.reshape(4, 4, 4, 2), ("x", "z", "y", "c"))
    zero = ("z", "y", "c")
    every = ("x", "z", "y", "c")
    rows = P(every, None)
    in_specs = (rows,) * 5 + (
        P("x", None, zero),
        P("x", zero),
        P("x", zero, None),
        P("x", None),
    )
    out_specs = (
        rows,
        rows,
        P("x", None, zero),
        P("x", zero),
        P("x", zero, None),
        P("x", None),
    )
    return jax.shard_map(
        on_device, mesh=fine, in_specs=in_specs, out_specs=out_specs, check_vma=False
    )
```

```python
import functools

import jax
import jax.numpy as jnp
from jax import lax
from jax.experimental import pallas as pl
from jax.experimental.pallas import tpu as pltpu
from jax.sharding import Mesh, PartitionSpec as P

BF = jnp.bfloat16
F32 = jnp.float32
EXTRA = 16
NT = (((1,), (1,)), ((), ()))
NN = (((1,), (0,)), ((), ()))
TN = (((0,), (0,)), ((), ()))


def dot(a, b, dims):
    return lax.dot_general(a, b, dims, preferred_element_type=F32)


def shift(value, axis, step):
    n = lax.axis_size(axis)
    return lax.ppermute(value, axis, [(i, (i + step) % n) for i in range(n)])


def shift_y(value, step, mirrored):
    n = lax.axis_size("y")
    moves = []
    for y in range(n):
        for c in range(2):
            to = (y + (-step if mirrored and c else step)) % n
            moves.append((2 * y + c, 2 * to + c))
    return lax.ppermute(value, ("y", "c"), moves)


def shape(rows, columns, dtype=BF):
    return jax.ShapeDtypeStruct((rows, columns), dtype)


def full(a):
    return pl.BlockSpec(a.shape, lambda i: (0,) * len(a.shape))


def lead(a, index):
    return pl.BlockSpec((1, *a.shape[1:]), lambda i: (index,) + (0,) * (len(a.shape) - 1))


def call(kernel, name, out_shape, operands, flops=0, scratch=(), vmem=8):
    pairs = [o if isinstance(o, tuple) else (o, None) for o in operands]
    size = sum(a.size * a.dtype.itemsize for a, _ in pairs)
    size += sum(s.size * s.dtype.itemsize for s in out_shape)
    return pl.pallas_call(
        kernel,
        out_shape=out_shape,
        grid=(1,),
        in_specs=[full(a) if k is None else lead(a, k) for a, k in pairs],
        out_specs=[full(s) for s in out_shape],
        scratch_shapes=scratch,
        compiler_params=pltpu.CompilerParams(vmem_limit_bytes=vmem * 1024 * 1024),
        cost_estimate=pl.CostEstimate(flops=flops, bytes_accessed=size, transcendentals=0),
        name=name,
    )(*[a for a, _ in pairs])


def call_loading(kernel, name, out_shape, arrays):
    n = len(arrays)

    def body(*refs):
        sources, outs = refs[:n], refs[n : n + len(out_shape)]
        copies, sems = refs[n + len(out_shape) : -1], refs[-1]
        moves = [
            pltpu.make_async_copy(a, b, sems.at[k])
            for k, (a, b) in enumerate(zip(sources, copies))
        ]
        for m in moves:
            m.start()
        for m in moves:
            m.wait()
        kernel(*copies, *outs)

    return pl.pallas_call(
        body,
        out_shape=out_shape,
        in_specs=[pl.BlockSpec(memory_space=pl.ANY)] * n,
        out_specs=[pl.BlockSpec(memory_space=pltpu.VMEM)] * len(out_shape),
        scratch_shapes=[pltpu.VMEM(a.shape, a.dtype) for a in arrays]
        + [pltpu.SemaphoreType.DMA((n,))],
        compiler_params=pltpu.CompilerParams(vmem_limit_bytes=56 * 1024 * 1024),
        name=name,
    )(*arrays)


def high_low(value):
    high = value.astype(BF).astype(F32)
    return [high, value - high]


def lines_of(lines, width, dtype):
    m = lines[0].shape[1]
    rest = EXTRA - sum(line.shape[0] for line in lines)
    block = jnp.concatenate(lines + [jnp.zeros((rest, m), F32)], axis=0)
    if m < width:
        block = jnp.concatenate([block, jnp.zeros((EXTRA, width - m), F32)], axis=1)
    return block.astype(dtype)


def share_kernel(w_in, b_in, w_out, out):
    units = w_out.shape[1]
    out[0:units] = w_in[0].astype(F32).T.astype(BF)
    out[units : units + EXTRA] = lines_of([b_in[...].astype(F32)], out.shape[1], BF)
    out[units + EXTRA :] = w_out[0]


def prepare_kernel(routes, slots, combine, tokens, grads, raw, places, *outs):
    n_expert = len(outs)
    cap = outs[0].shape[0]
    n_tok = tokens.shape[0]
    turned = routes[...] - lax.axis_index("x")
    turned = jnp.where(turned < 0, turned + n_expert, turned)
    place = jnp.where(slots[...] < cap, turned * cap + slots[...], -1)
    places[...] = place
    raw[0:n_tok] = grads[...]
    side = [place.astype(F32), combine[...].astype(F32)]
    raw[n_tok:] = lines_of(side, grads.shape[1], BF)
    spots = lax.broadcasted_iota(jnp.int32, (n_expert * cap, n_tok), 0)
    picks = jnp.where((place[0:1, :] == spots) | (place[1:2, :] == spots), 1.0, 0.0)
    rows = dot(picks.astype(BF), tokens[...], NN).astype(BF)
    for s, out in enumerate(outs):
        out[...] = rows[s * cap : (s + 1) * cap]


def douts_kernel(own, below, above, far, *outs):
    cap = outs[0].shape[1]
    n_tok = own.shape[0] - EXTRA
    for z, raw in enumerate((own[...], below[...], above[...], far[...])):
        side = raw[n_tok : n_tok + 4, 0:n_tok].astype(F32)
        spots = lax.broadcasted_iota(jnp.int32, (len(outs) * cap, n_tok), 0)
        place = side[0:2].astype(jnp.int32)
        picks = jnp.where(place[0:1] == spots, side[2:3], 0.0)
        picks = picks + jnp.where(place[1:2] == spots, side[3:4], 0.0)
        rows = dot(picks.astype(BF), raw[0:n_tok], NN).astype(BF)
        for s, out in enumerate(outs):
            out[z] = rows[s * cap : (s + 1) * cap]


def rows_kernel(n_x, n_z, n_d, with_bias, *refs):
    n_d = n_z * n_d
    xs, ds = refs[:n_x], refs[n_x : n_x + n_d]
    mine, other, direct, mirror, far_w, b_out, *outs = refs[n_x + n_d :]
    x, d, dpre, hidden, *dxs = outs
    shares = [
        (mine, other),
        (direct.at[0], direct.at[1]),
        (mirror.at[1], mirror.at[0]),
        (far_w.at[0], far_w.at[1]),
    ]
    width = x.shape[1]
    for parts, whole in ((xs, x), (ds, d)):
        at = 0
        for p in parts:
            count = p.shape[-2]
            whole[at : at + count] = p[...].reshape(count, width)
            at += count
    n_y = len(shares)
    unit = (mine.shape[0] - EXTRA) // 2
    xb = x[...]
    db = d[...]

    def w_in_of(k):
        return jnp.concatenate([r[0:unit] for r in shares[k]], axis=0)

    def dots(k):
        bias = jnp.concatenate([r[unit : unit + 1, 0:unit] for r in shares[k]], axis=1)
        w_out = jnp.concatenate([r[unit + EXTRA :] for r in shares[k]], axis=0)
        return dot(xb, w_in_of(k), NT) + bias.astype(F32), dot(db, w_out, NT)

    term = total = grad = None
    now = dots(0)
    for k in range(n_y):
        pre, back = now
        if k + 1 < n_y:
            now = dots(k + 1)
        cdf = 0.5 * (1.0 + lax.erf(pre * 0.7071067811865476))
        dens = jnp.exp(-0.5 * pre * pre) * 0.3989422804014327
        hidden32 = pre * cdf
        new = (back * (cdf + pre * dens)).astype(BF)
        hid = hidden32.astype(BF)
        for c in range(2):
            dpre[c, :, k * unit : (k + 1) * unit] = new[:, c * unit : (c + 1) * unit]
            hidden[c, :, k * unit : (k + 1) * unit] = hid[:, c * unit : (c + 1) * unit]
        by_row = hidden32 * back
        term = by_row if k == 0 else term + by_row
        if k > 0:
            part = dot(grad, w_in_of(k - 1), NN)
            total = part if k == 1 else total + part
        grad = new
    total = total + dot(grad, w_in_of(n_y - 1), NN)
    line = jnp.sum(term.T, axis=0, keepdims=True)
    m = x.shape[0] // n_z
    if n_z == 1:
        low, high = dxs
        cut = low.shape[0]
        low[...] = total[0:cut].astype(BF)
        high[0 : m - cut] = total[cut:].astype(BF)
        high[m - cut :] = lines_of(high_low(line), width, BF)
    else:
        for z, out in enumerate(dxs):
            out[0:m] = total[z * m : (z + 1) * m]
            own = line[:, z * m : (z + 1) * m]
            if z == 0:
                by_bias = (d[0:m].astype(F32) * b_out[...].astype(F32)).T
                own = own + jnp.sum(by_bias, axis=0, keepdims=True)
            out[m:] = lines_of([own], width, F32)


def rows_set(xs, ds, w, b_out):
    n_z = len(ds)
    width = b_out.shape[1]
    m = sum(a.shape[0] for a in xs)
    units = 4 * (w[0].shape[0] - EXTRA)
    part = jax.ShapeDtypeStruct((2, m, units // 2), BF)
    if n_z == 1:
        dxs = [shape(m // 2, width), shape(m // 2 + EXTRA, width)]
    else:
        dxs = [shape(m // n_z + EXTRA, width, F32)] * n_z
    return call(
        functools.partial(rows_kernel, len(xs), n_z, len(ds[0]), n_z > 1),
        "rows",
        [shape(m, width), shape(m, width), part, part, *dxs],
        [*xs, *[p for z in ds for p in z], *w, b_out],
        flops=6 * m * units * width,
        vmem=14 if n_z == 1 else 28,
    )


def weights_sums(n_sets, refs):
    xs, ds, dpres, hiddens = (refs[k * n_sets : (k + 1) * n_sets] for k in range(4))
    grad_in = sum(dot(p[0], x[...], TN) for p, x in zip(dpres, xs))
    grad_out = sum(dot(h[0], d[...], TN) for h, d in zip(hiddens, ds))
    sum_in = sum(jnp.sum(p[0].astype(F32), axis=0, keepdims=True) for p in dpres)
    sum_out = sum(jnp.sum(d[...].astype(F32), axis=0, keepdims=True) for d in ds)
    gap = jnp.zeros((1, sum_out.shape[1] - sum_in.shape[1]), F32)
    return grad_in, grad_out, jnp.concatenate([sum_in, gap], axis=1), sum_out


def away_kernel(n_sets, *refs):
    out = refs[4 * n_sets]
    grad_in, grad_out, sum_in, sum_out = weights_sums(n_sets, refs)
    units = grad_in.shape[0]
    out[0:units] = grad_in.astype(BF)
    out[units : 2 * units] = grad_out.astype(BF)
    out[2 * units :] = lines_of(high_low(sum_in) + high_low(sum_out), out.shape[1], BF)


def home_kernel(n_sets, *refs):
    got, *outs = refs[4 * n_sets :]
    grad_in, grad_out, sum_in, sum_out = weights_sums(n_sets, refs)
    units, width = grad_in.shape
    side = got[2 * units : 2 * units + 4].astype(F32)
    sum_out = sum_out + side[2:3] + side[3:4]
    side = side[0:1] + side[1:2]
    n_y = len(outs)
    unit = units // n_y
    for k, out in enumerate(outs):
        here = slice(k * unit, (k + 1) * unit)
        there = (0, 2, 1, 3)[k] * unit
        line = sum_in[:, here] + side[:, there : there + unit]
        line = jnp.concatenate([line, jnp.zeros((1, width - unit), F32)], axis=1)
        total = grad_in[here] + got[there : there + unit].astype(F32)
        out[0:unit] = total.astype(out.dtype)
        total = grad_out[here] + got[units + there : units + there + unit].astype(F32)
        out[unit : 2 * unit] = total.astype(out.dtype)
        if k == 0:
            lines = [line, jnp.zeros_like(line), sum_out]
        else:
            lines = high_low(line) + high_low(sum_out)
        out[2 * unit :] = lines_of(lines, width, out.dtype)


def weights_part(sets, core, got):
    x, d, dpre, hidden = zip(*sets)
    width = x[0].shape[1]
    units = dpre[0].shape[2]
    n_y = 4
    operands = [*x, *d, *[(p, core) for p in dpre], *[(h, core) for h in hidden]]
    flops = 4 * sum(a.shape[0] for a in x) * units * width
    if got is None:
        kernel = functools.partial(away_kernel, len(sets))
        out = [shape(2 * units + EXTRA, width)]
        return call(kernel, "away", out, operands, flops, vmem=20)[0]
    unit = units // n_y
    return call(
        functools.partial(home_kernel, len(sets)),
        "home",
        [shape(2 * unit + EXTRA, width, BF if r else F32) for r in range(n_y)],
        [*operands, got],
        flops,
        vmem=24,
    )


def last_kernel(own, a, b, c, grad_in, grad_bias_in, grad_out, grad_bias_out):
    units = grad_out.shape[1]
    total = own[...] + a[...].astype(F32) + b[...].astype(F32) + c[...].astype(F32)
    grad_in[0] = total[0:units].T.astype(BF)
    grad_out[0] = total[units : 2 * units].astype(BF)
    tail = total[2 * units :]
    grad_bias_in[...] = (tail[0:1] + tail[1:2])[:, 0:units]
    grad_bias_out[...] = tail[2:3] + tail[3:4]


def join_kernel(below, above, got_below, got_above, out_below, out_above):
    m = below.shape[0] - EXTRA
    width = below.shape[1]
    cut = got_above.shape[0]
    out_above[0:cut] = (above[0:cut] + got_above[...].astype(F32)).astype(BF)
    out_above[cut:m] = above[cut:m].astype(BF)
    out_above[m:] = lines_of(high_low(above[m : m + 1]), width, BF)
    out_below[0:cut] = below[0:cut].astype(BF)
    out_below[cut:m] = (below[cut:m] + got_below[0 : m - cut].astype(F32)).astype(BF)
    side = got_below[m - cut : m - cut + 2].astype(F32)
    out_below[m:] = lines_of(high_low(below[m : m + 1] + side[0:1] + side[1:2]), width, BF)


def sum_kernel(own, a, b, out):
    n_expert = out.shape[0]
    here = lax.axis_index("x")
    m = own.shape[0] - EXTRA
    total = own[...] + a[...].astype(F32) + b[...].astype(F32)
    lines = lines_of(high_low(total[m : m + 1] + total[m + 1 : m + 2]), own.shape[1], BF)
    cap = m // n_expert
    for s in range(n_expert):
        to = lax.rem(here + (n_expert - s), n_expert)
        out[to, 0:cap] = total[s * cap : (s + 1) * cap].astype(BF)
        out[to, cap:] = lines


def finish_kernel(places, weights, pieces, out, by_weight):
    n_expert = pieces.shape[0]
    cap = pieces.shape[1] - EXTRA
    n_tok = places.shape[1]
    here = lax.axis_index("x")
    total = None
    sums = [None, None]
    spots = lax.broadcasted_iota(jnp.int32, (n_expert * cap, n_tok), 0)
    picks = [jnp.where(places[k : k + 1, :] == spots, 1.0, 0.0) for k in range(2)]
    both = (picks[0] + picks[1]).astype(BF)
    for s in range(n_expert):
        piece = pieces.at[lax.rem(here + s, n_expert)]
        part = dot(both[s * cap : (s + 1) * cap], piece[0:cap], TN)
        total = part if total is None else total + part
        inside = (spots >= s * cap) & (spots < (s + 1) * cap)
        for k in range(2):
            pick = jnp.where(inside, picks[k], 0.0).astype(BF)
            found = dot(piece[cap:, 0 : n_expert * cap], pick, NN)
            line = found[0:1] + found[1:2]
            sums[k] = line if sums[k] is None else sums[k] + line
    out[...] = total.astype(BF)
    by_weight[...] = jnp.concatenate(sums, axis=0) / weights[...].astype(F32)


def on_device(tokens, grads_out, routes, slots, combine, w_in, b_in, w_out, b_out):
    n_expert = lax.axis_size("x")
    tok_rows, width = tokens.shape
    cap = 2 * tok_rows // n_expert
    units = w_in.shape[2]

    barrier = lax.optimization_barrier

    raw, places, *x_sent = call_loading(
        prepare_kernel,
        "prepare",
        [shape(tok_rows + EXTRA, width), shape(2, tok_rows, jnp.int32)]
        + [shape(cap, width)] * n_expert,
        [routes.T, slots.T, combine.T, tokens, grads_out],
    )
    raw_below = shift(raw, "z", 1)
    raw_above = shift(raw, "z", -1)
    x_got = [x_sent[0]] + [shift(x_sent[s], "x", s) for s in range(1, n_expert)]
    raw_below, raw_above, w_in, w_out, b_in, *x_got = barrier(
        (raw_below, raw_above, w_in, w_out, b_in, *x_got)
    )

    raw_far = shift(raw_below, "z", 1)
    mine = call_loading(
        share_kernel, "share", [shape(2 * units + EXTRA, width)], [w_in, b_in, w_out]
    )[0]
    other = shift(mine, "c", 1)
    x_own = jnp.concatenate(x_got, axis=0)
    both = jnp.stack([mine, other])
    x_own, raw_far, both = barrier((x_own, raw_far, both))

    d_sent = call(
        douts_kernel,
        "douts",
        [jax.ShapeDtypeStruct((4, cap, width), BF)] * n_expert,
        [raw, raw_below, raw_above, raw_far],
    )
    x_below = shift(x_own, "z", 1)
    x_above = shift(x_own, "z", -1)
    direct = shift_y(both, 1, True)
    d_1 = shift(d_sent[1], "x", 1)
    d_3 = shift(d_sent[3], "x", -1)
    x_below, x_above, direct, d_1, d_3, d_2 = barrier(
        (x_below, x_above, direct, d_1, d_3, d_sent[2])
    )

    d_2 = shift(d_2, "x", 2)
    far_w = shift_y(direct, 1, True)
    x_far = shift(x_below, "z", 1)
    mirror = shift(direct, "c", 1)
    d = [d_sent[0], d_1, d_2, d_3]
    w = [mine, other, direct, mirror, far_w]

    far = rows_set([x_far], [[(a, 3) for a in d]], w, b_out)
    x_own, low, high = lax.optimization_barrier((x_own, far[4], far[5]))
    got_above = shift(low, "z", 1)
    got_below = shift(high, "z", -1)
    near = rows_set([x_own, x_below, x_above], [[(a, z) for a in d] for z in range(3)], w, b_out)
    sets = [far[:4], near[:4]]

    away = weights_part(sets, 1, None)
    away, got_above, got_below = lax.optimization_barrier((away, got_above, got_below))
    home = weights_part(sets, 0, shift(away, "c", 1))

    own, below, above = near[4:]
    like = shape(*own.shape)
    out_below, out_above = call(
        join_kernel, "join", [like, like], [below, above, got_below, got_above]
    )
    parts = [shift(out_above, "z", 1), shift(out_below, "z", -1)]
    like = jax.ShapeDtypeStruct((n_expert, cap + EXTRA, width), BF)
    pieces = call(sum_kernel, "sum_z", [like], [own, *parts])[0]
    final = lax.all_to_all(pieces, "x", 0, 0, tiled=True)
    moved = [
        shift_y(home[3], 2, False),
        shift_y(home[1], -1, True),
        shift_y(home[2], 1, True),
    ]
    grad_tokens, by_weight = call(
        finish_kernel,
        "finish",
        [shape(tok_rows, width), shape(2, tok_rows, F32)],
        [places, combine.T, final],
    )
    grad_w_in, grad_b_in, grad_w_out, grad_b_out = call(
        last_kernel,
        "last",
        [
            jax.ShapeDtypeStruct(w_in.shape, BF),
            shape(1, units, F32),
            jax.ShapeDtypeStruct(w_out.shape, BF),
            shape(1, width, F32),
        ],
        [home[0], *moved],
    )
    return (grad_tokens, by_weight.T, grad_w_in, grad_b_in, grad_w_out, grad_b_out)


def solution(mesh):
    fine = Mesh(mesh.devices.reshape(4, 4, 4, 2), ("x", "z", "y", "c"))
    zero = ("z", "y", "c")
    rows = P(("x", "z", "y", "c"), None)
    in_specs = (rows,) * 5 + (
        P("x", None, zero),
        P("x", zero),
        P("x", zero, None),
        P("x", None),
    )
    out_specs = (rows, rows) + in_specs[5:]
    return jax.shard_map(
        on_device, mesh=fine, in_specs=in_specs, out_specs=out_specs, check_vma=False
    )
```

```python
import functools

import jax
import jax.numpy as jnp
from jax import lax
from jax.experimental import pallas as pl
from jax.experimental.pallas import tpu as pltpu
from jax.sharding import Mesh, PartitionSpec as P

BF = jnp.bfloat16
F32 = jnp.float32
EXTRA = 16
NT = (((1,), (1,)), ((), ()))
NN = (((1,), (0,)), ((), ()))
TN = (((0,), (0,)), ((), ()))


def dot(a, b, dims):
    return lax.dot_general(a, b, dims, preferred_element_type=F32)


def shift(value, axis, step):
    n = lax.axis_size(axis)
    return lax.ppermute(value, axis, [(i, (i + step) % n) for i in range(n)])


def shift_y(value, step, mirrored):
    n = lax.axis_size("y")
    moves = []
    for y in range(n):
        for c in range(2):
            to = (y + (-step if mirrored and c else step)) % n
            moves.append((2 * y + c, 2 * to + c))
    return lax.ppermute(value, ("y", "c"), moves)


def shape(rows, columns, dtype=BF):
    return jax.ShapeDtypeStruct((rows, columns), dtype)


def full(a):
    return pl.BlockSpec(a.shape, lambda i: (0,) * len(a.shape))


def span(a, first, rows):
    return pl.BlockSpec((rows, a.shape[1]), lambda i: (first // rows, 0))


def lead(a, index):
    return pl.BlockSpec((1, *a.shape[1:]), lambda i: (index,) + (0,) * (len(a.shape) - 1))


def call(kernel, name, out_shape, operands, flops=0, scratch=(), vmem=8):
    parts = [o if isinstance(o, tuple) else (o,) for o in operands]
    size = sum(p[0].size * p[0].dtype.itemsize for p in parts)
    size += sum(s.size * s.dtype.itemsize for s in out_shape)
    return pl.pallas_call(
        kernel,
        out_shape=out_shape,
        grid=(1,),
        in_specs=[(full, lead, span)[len(p) - 1](*p) for p in parts],
        out_specs=[full(s) for s in out_shape],
        scratch_shapes=scratch,
        compiler_params=pltpu.CompilerParams(vmem_limit_bytes=vmem * 1024 * 1024),
        cost_estimate=pl.CostEstimate(flops=flops, bytes_accessed=size, transcendentals=0),
        name=name,
    )(*[p[0] for p in parts])


def call_loading(kernel, name, out_shape, arrays):
    n = len(arrays)

    def body(*refs):
        sources, outs = refs[:n], refs[n : n + len(out_shape)]
        copies, sems = refs[n + len(out_shape) : -1], refs[-1]
        moves = [
            pltpu.make_async_copy(a, b, sems.at[k])
            for k, (a, b) in enumerate(zip(sources, copies))
        ]
        for m in moves:
            m.start()
        for m in moves:
            m.wait()
        kernel(*copies, *outs)

    return pl.pallas_call(
        body,
        out_shape=out_shape,
        in_specs=[pl.BlockSpec(memory_space=pl.ANY)] * n,
        out_specs=[pl.BlockSpec(memory_space=pltpu.VMEM)] * len(out_shape),
        scratch_shapes=[pltpu.VMEM(a.shape, a.dtype) for a in arrays]
        + [pltpu.SemaphoreType.DMA((n,))],
        compiler_params=pltpu.CompilerParams(vmem_limit_bytes=56 * 1024 * 1024),
        name=name,
    )(*arrays)


def high_low(value):
    high = value.astype(BF).astype(F32)
    return [high, value - high]


def lines_of(lines, width, dtype):
    m = lines[0].shape[1]
    rest = EXTRA - sum(line.shape[0] for line in lines)
    block = jnp.concatenate(lines + [jnp.zeros((rest, m), F32)], axis=0)
    if m < width:
        block = jnp.concatenate([block, jnp.zeros((EXTRA, width - m), F32)], axis=1)
    return block.astype(dtype)


def prepare_kernel(
    routes, slots, combine, tokens, grads, w_in, b_in, w_out, share, raw, places, *outs
):
    units = w_out.shape[1]
    share[0:units] = w_in[0].astype(F32).T.astype(BF)
    share[units : units + EXTRA] = lines_of([b_in[...].astype(F32)], share.shape[1], BF)
    share[units + EXTRA :] = w_out[0]
    n_expert = len(outs)
    cap = outs[0].shape[0]
    n_tok = tokens.shape[0]
    turned = routes[...] - lax.axis_index("x")
    turned = jnp.where(turned < 0, turned + n_expert, turned)
    place = jnp.where(slots[...] < cap, turned * cap + slots[...], -1)
    places[...] = place
    raw[0:n_tok] = grads[...]
    side = [place.astype(F32), combine[...].astype(F32)]
    raw[n_tok:] = lines_of(side, grads.shape[1], BF)
    spots = lax.broadcasted_iota(jnp.int32, (n_expert * cap, n_tok), 0)
    picks = jnp.where((place[0:1, :] == spots) | (place[1:2, :] == spots), 1.0, 0.0)
    rows = dot(picks.astype(BF), tokens[...], NN).astype(BF)
    for s, out in enumerate(outs):
        out[...] = rows[s * cap : (s + 1) * cap]


def douts_kernel(own, below, above, far, *outs):
    cap = outs[0].shape[1]
    n_tok = own.shape[0] - EXTRA
    for z, raw in enumerate((own[...], below[...], above[...], far[...])):
        side = raw[n_tok : n_tok + 4, 0:n_tok].astype(F32)
        spots = lax.broadcasted_iota(jnp.int32, (len(outs) * cap, n_tok), 0)
        place = side[0:2].astype(jnp.int32)
        picks = jnp.where(place[0:1] == spots, side[2:3], 0.0)
        picks = picks + jnp.where(place[1:2] == spots, side[3:4], 0.0)
        rows = dot(picks.astype(BF), raw[0:n_tok], NN).astype(BF)
        for s, out in enumerate(outs):
            out[z] = rows[s * cap : (s + 1) * cap]


def rows_kernel(n_x, n_d, blocks, *refs):
    xs, ds = refs[:n_x], refs[n_x : n_x + n_d]
    mine, other, direct, mirror, far_w, b_out, *outs = refs[n_x + n_d :]
    x, d, dpre, hidden, *dxs = outs
    shares = [
        (mine, other),
        (direct.at[0], direct.at[1]),
        (mirror.at[1], mirror.at[0]),
        (far_w.at[0], far_w.at[1]),
    ]
    width = x.shape[1]
    for parts, whole in ((xs, x), (ds, d)):
        at = 0
        for p in parts:
            count = p.shape[-2]
            whole[at : at + count] = p[...].reshape(count, width)
            at += count
    n_y = len(shares)
    unit = (mine.shape[0] - EXTRA) // 2
    xb = x[...]
    db = d[...]

    def w_in_of(k):
        return jnp.concatenate([r[0:unit] for r in shares[k]], axis=0)

    def dots(k):
        bias = jnp.concatenate([r[unit : unit + 1, 0:unit] for r in shares[k]], axis=1)
        w_out = jnp.concatenate([r[unit + EXTRA :] for r in shares[k]], axis=0)
        return dot(xb, w_in_of(k), NT) + bias.astype(F32), dot(db, w_out, NT)

    term = total = grad = None
    now = dots(0)
    for k in range(n_y):
        pre, back = now
        if k + 1 < n_y:
            now = dots(k + 1)
        cdf = 0.5 * (1.0 + lax.erf(pre * 0.7071067811865476))
        dens = jnp.exp(-0.5 * pre * pre) * 0.3989422804014327
        hidden32 = pre * cdf
        new = (back * (cdf + pre * dens)).astype(BF)
        hid = hidden32.astype(BF)
        for c in range(2):
            dpre[c, :, k * unit : (k + 1) * unit] = new[:, c * unit : (c + 1) * unit]
            hidden[c, :, k * unit : (k + 1) * unit] = hid[:, c * unit : (c + 1) * unit]
        by_row = hidden32 * back
        term = by_row if k == 0 else term + by_row
        if k > 0:
            part = dot(grad, w_in_of(k - 1), NN)
            total = part if k == 1 else total + part
        grad = new
    total = total + dot(grad, w_in_of(n_y - 1), NN)
    line = jnp.sum(term.T, axis=0, keepdims=True)
    at = 0
    for (count, is_own), out in zip(blocks, dxs):
        out[0:count] = total[at : at + count].astype(out.dtype)
        here = line[:, at : at + count]
        if is_own:
            by_bias = (d[at : at + count].astype(F32) * b_out[...].astype(F32)).T
            here = here + jnp.sum(by_bias, axis=0, keepdims=True)
            out[count:] = lines_of([here], width, F32)
        else:
            out[count:] = lines_of(high_low(here), width, BF)
        at += count


def rows_set(xs, ds, blocks, w, b_out):
    width = b_out.shape[1]
    m = sum(count for count, _ in blocks)
    units = 4 * (w[0].shape[0] - EXTRA)
    part = jax.ShapeDtypeStruct((2, m, units // 2), BF)
    dxs = [shape(count + EXTRA, width, F32 if own else BF) for count, own in blocks]
    return call(
        functools.partial(rows_kernel, len(xs), len(ds), blocks),
        "rows",
        [shape(m, width), shape(m, width), part, part, *dxs],
        [*xs, *ds, *w, b_out],
        flops=6 * m * units * width,
        vmem=26,
    )


def sums_kernel(x, d, dpre, hidden, out):
    for c in range(2):
        grads = weight_sums(x[...], d[...], dpre[c], hidden[c])
        at = 0
        for g in grads:
            out[c, at : at + g.shape[0]] = g
            at += g.shape[0]


def weight_sums(x, d, dpre, hidden):
    grad_in = dot(dpre, x, TN)
    grad_out = dot(hidden, d, TN)
    line_in = jnp.sum(dpre.astype(F32), axis=0, keepdims=True)
    line_out = jnp.sum(d.astype(F32), axis=0, keepdims=True)
    line_in = jnp.concatenate(
        [line_in, jnp.zeros((1, d.shape[1] - dpre.shape[1]), F32)], axis=1
    )
    return grad_in, grad_out, lines_of([line_in, line_out], d.shape[1], F32)


def away_kernel(near, x, d, dpre, hidden, out):
    grad_in, grad_out, lines = weight_sums(x[...], d[...], dpre[0], hidden[0])
    units = grad_in.shape[0]
    out[0:units] = (near[0, 0:units] + grad_in).astype(BF)
    out[units : 2 * units] = (near[0, units : 2 * units] + grad_out).astype(BF)
    lines = near[0, 2 * units :] + lines
    out[2 * units :] = lines_of(high_low(lines[0:1]) + high_low(lines[1:2]), out.shape[1], BF)


def home_kernel(near, x, d, dpre, hidden, out):
    at = 0
    for g in weight_sums(x[...], d[...], dpre[0], hidden[0]):
        rows = slice(at, at + g.shape[0])
        out[rows] = near[0, rows] + g
        at += g.shape[0]


def merge_kernel(own, got, *outs):
    units = (own.shape[0] - EXTRA) // 2
    width = own.shape[1]
    lines = own[2 * units : 2 * units + 2]
    side = got[2 * units : 2 * units + 4].astype(F32)
    sum_out = lines[1:2] + side[2:3] + side[3:4]
    side = side[0:1] + side[1:2]
    n_y = len(outs)
    unit = units // n_y
    for k, out in enumerate(outs):
        here = k * unit
        there = (0, 2, 1, 3)[k] * unit
        line = lines[0:1, here : here + unit] + side[:, there : there + unit]
        line = jnp.concatenate([line, jnp.zeros((1, width - unit), F32)], axis=1)
        for at in (0, unit):
            rows = slice(at, at + unit)
            here_at, there_at = n_y * at + here, n_y * at + there
            total = own[here_at : here_at + unit] + got[there_at : there_at + unit].astype(F32)
            out[rows] = total.astype(out.dtype)
        if k == 0:
            both = [line, jnp.zeros_like(line), sum_out]
        else:
            both = high_low(line) + high_low(sum_out)
        out[2 * unit :] = lines_of(both, width, out.dtype)


def last_kernel(own, a, b, c, grad_in, grad_bias_in, grad_out, grad_bias_out):
    units = grad_out.shape[1]
    total = own[...] + a[...].astype(F32) + b[...].astype(F32) + c[...].astype(F32)
    grad_in[0] = total[0:units].T.astype(BF)
    grad_out[0] = total[units : 2 * units].astype(BF)
    tail = total[2 * units :]
    grad_bias_in[...] = (tail[0:1] + tail[1:2])[:, 0:units]
    grad_bias_out[...] = tail[2:3] + tail[3:4]


ORDER = (0, 1, 3, 2)


def sum_kernel(n_early, *refs):
    early, late, (far, out) = refs[:3], refs[3:6], refs[6:]
    n_expert = out.shape[0]
    here = lax.axis_index("x")
    width = far.shape[1]
    m = far.shape[0] - EXTRA
    cap = m // n_expert
    e = sum(r[...].astype(F32) for r in early)
    t = sum(r[...].astype(F32) for r in late)
    cut = n_early * cap
    line = [v[n : n + 1, 0:n] + v[n + 1 : n + 2, 0:n] for v, n in ((e, cut), (t, m - cut))]
    side = far[m : m + 2].astype(F32)
    line = jnp.concatenate(line, axis=1) + side[0:1, 0:m] + side[1:2, 0:m]
    lines = lines_of(high_low(line), width, BF)
    for k, s in enumerate(ORDER):
        to = lax.rem(here + (n_expert - s), n_expert)
        rows = slice(k * cap, (k + 1) * cap)
        total = e[rows] if k < n_early else t[k * cap - cut : (k + 1) * cap - cut]
        out[to, 0:cap] = (total + far[rows].astype(F32)).astype(BF)
        out[to, cap:] = lines


def finish_kernel(places, weights, pieces, out, by_weight):
    n_expert = pieces.shape[0]
    cap = pieces.shape[1] - EXTRA
    n_tok = places.shape[1]
    here = lax.axis_index("x")
    total = None
    sums = [None, None]
    spots = lax.broadcasted_iota(jnp.int32, (n_expert * cap, n_tok), 0)
    picks = [jnp.where(places[k : k + 1, :] == spots, 1.0, 0.0) for k in range(2)]
    both = (picks[0] + picks[1]).astype(BF)
    for s in range(n_expert):
        piece = pieces.at[lax.rem(here + s, n_expert)]
        part = dot(both[s * cap : (s + 1) * cap], piece[0:cap], TN)
        total = part if total is None else total + part
        lane = spots - ORDER.index(s) * cap
        inside = (lane >= 0) & (lane < cap)
        for k in range(2):
            pick = inside & (places[k : k + 1, :] == lane + s * cap)
            pick = jnp.where(pick, 1.0, 0.0).astype(BF)
            found = dot(piece[cap:, 0 : n_expert * cap], pick, NN)
            line = found[0:1] + found[1:2]
            sums[k] = line if sums[k] is None else sums[k] + line
    out[...] = total.astype(BF)
    by_weight[...] = jnp.concatenate(sums, axis=0) / weights[...].astype(F32)


def on_device(tokens, grads_out, routes, slots, combine, w_in, b_in, w_out, b_out):
    n_expert = lax.axis_size("x")
    tok_rows, width = tokens.shape
    cap = 2 * tok_rows // n_expert
    units = w_in.shape[2]

    barrier = lax.optimization_barrier

    mine, raw, places, *x_sent = call_loading(
        prepare_kernel,
        "prepare",
        [
            shape(2 * units + EXTRA, width),
            shape(tok_rows + EXTRA, width),
            shape(2, tok_rows, jnp.int32),
        ]
        + [shape(cap, width)] * n_expert,
        [routes.T, slots.T, combine.T, tokens, grads_out, w_in, b_in, w_out],
    )
    raw_below = shift(raw, "z", 1)
    raw_above = shift(raw, "z", -1)
    x_1 = shift(x_sent[1], "x", 1)
    x_3 = shift(x_sent[3], "x", -1)
    other = shift(mine, "c", 1)
    raw_below, raw_above, x_1, x_2, x_3 = barrier((raw_below, raw_above, x_1, x_sent[2], x_3))
    direct = shift_y(jnp.stack([mine, other]), 1, True)

    raw_far = shift(raw_below, "z", 1)
    x_own = jnp.concatenate([x_sent[0], x_1, x_3, shift(x_2, "x", 2)], axis=0)
    x_own, raw_far, direct = barrier((x_own, raw_far, direct))

    d_sent = call(
        douts_kernel,
        "douts",
        [jax.ShapeDtypeStruct((4, cap, width), BF)] * n_expert,
        [raw, raw_below, raw_above, raw_far],
    )
    x_below = shift(x_own, "z", 1)
    x_above = shift(x_own, "z", -1)
    far_w = shift_y(direct, 1, True)
    d_1 = shift(d_sent[1], "x", 1)
    d_3 = shift(d_sent[3], "x", -1)
    x_below, x_above, direct, far_w, d_1, d_3, d_2 = barrier(
        (x_below, x_above, direct, far_w, d_1, d_3, d_sent[2])
    )
    mirror = shift(direct, "c", 1)
    w = [mine, other, direct, mirror, far_w]

    d_2 = shift(d_2, "x", 2)
    half = x_own.shape[0] // 2
    x_far_a = shift(x_below[:half], "z", 1)
    x_far_b = shift(x_above[half:], "z", -1)
    n_early = 3
    cut = n_early * cap
    sides = (x_own, x_below, x_above)
    early = rows_set(
        [(a, 0, cut) for a in sides],
        [(a, z) for z in range(3) for a in (d_sent[0], d_1, d_3)],
        [(cut, True), (cut, False), (cut, False)],
        w,
        b_out,
    )
    acc = call(
        sums_kernel,
        "sums",
        [jax.ShapeDtypeStruct((2, 8 * units + EXTRA, width), F32)],
        early[:4],
        flops=8 * 3 * cut * 4 * units * width,
        vmem=28,
    )[0]
    early_above = shift(early[6], "z", 1)
    early_below = shift(early[5], "z", -1)
    d_2, x_far_a, x_far_b, acc = barrier((d_2, x_far_a, x_far_b, acc))
    late = rows_set(
        [(a, cut, cap) for a in sides] + [x_far_a, x_far_b],
        [(d_2, z) for z in range(3)] + [(a, 3) for a in (d_sent[0], d_1, d_3, d_2)],
        [(cap, True), (cap, False), (cap, False), (n_expert * cap, False)],
        w,
        b_out,
    )

    ends = [late[0], late[1], late[2], late[3]]
    flops = 4 * 7 * cap * 4 * units * width
    out = shape(8 * units + EXTRA, width)
    operands = [(acc, 1), *ends[:2], (late[2], 1), (late[3], 1)]
    away = call(away_kernel, "away", [out], operands, flops, vmem=20)[0]
    away, early_above, early_below = barrier((away, early_above, early_below))
    got = shift(away, "c", 1)
    out = shape(8 * units + EXTRA, width, F32)
    operands = [(acc, 0), *ends[:2], (late[2], 0), (late[3], 0)]
    home = call(home_kernel, "home", [out], operands, flops, vmem=24)[0]
    home = call(
        merge_kernel,
        "merge",
        [shape(2 * units + EXTRA, width, BF if k else F32) for k in range(4)],
        [home, got],
        vmem=16,
    )

    far = shift(late[7], "z", 2)
    late_above = shift(late[6], "z", 1)
    late_below = shift(late[5], "z", -1)
    pieces = call(
        functools.partial(sum_kernel, n_early),
        "sum_z",
        [jax.ShapeDtypeStruct((n_expert, cap + EXTRA, width), BF)],
        [early[4], early_above, early_below, late[4], late_above, late_below, far],
    )[0]
    final = lax.all_to_all(pieces, "x", 0, 0, tiled=True)
    moved = [
        shift_y(home[3], 2, False),
        shift_y(home[1], -1, True),
        shift_y(home[2], 1, True),
    ]
    grad_tokens, by_weight = call(
        finish_kernel,
        "finish",
        [shape(tok_rows, width), shape(2, tok_rows, F32)],
        [places, combine.T, final],
    )
    grad_w_in, grad_b_in, grad_w_out, grad_b_out = call(
        last_kernel,
        "last",
        [
            jax.ShapeDtypeStruct(w_in.shape, BF),
            shape(1, units, F32),
            jax.ShapeDtypeStruct(w_out.shape, BF),
            shape(1, width, F32),
        ],
        [home[0], *moved],
    )
    return (grad_tokens, by_weight.T, grad_w_in, grad_b_in, grad_w_out, grad_b_out)


def solution(mesh):
    fine = Mesh(mesh.devices.reshape(4, 4, 4, 2), ("x", "z", "y", "c"))
    zero = ("z", "y", "c")
    rows = P(("x", "z", "y", "c"), None)
    in_specs = (rows,) * 5 + (
        P("x", None, zero),
        P("x", zero),
        P("x", zero, None),
        P("x", None),
    )
    out_specs = (rows, rows) + in_specs[5:]
    return jax.shard_map(
        on_device, mesh=fine, in_specs=in_specs, out_specs=out_specs, check_vma=False
    )
```

```python
import functools

import jax
import jax.numpy as jnp
from jax import lax
from jax.experimental import pallas as pl
from jax.experimental.pallas import tpu as pltpu
from jax.sharding import Mesh, PartitionSpec as P

BF = jnp.bfloat16
F32 = jnp.float32
EXTRA = 16
NT = (((1,), (1,)), ((), ()))
NN = (((1,), (0,)), ((), ()))
TN = (((0,), (0,)), ((), ()))


def dot(a, b, dims):
    return lax.dot_general(a, b, dims, preferred_element_type=F32)


def shift(value, axis, step):
    n = lax.axis_size(axis)
    return lax.ppermute(value, axis, [(i, (i + step) % n) for i in range(n)])


def shape(rows, columns, dtype=BF):
    return jax.ShapeDtypeStruct((rows, columns), dtype)


def full(a):
    return pl.BlockSpec(a.shape, lambda i: (0,) * len(a.shape))


def span(a, first, rows):
    return pl.BlockSpec((rows, a.shape[1]), lambda i: (first // rows, 0))


def lead(a, index):
    return pl.BlockSpec((1, *a.shape[1:]), lambda i: (index,) + (0,) * (len(a.shape) - 1))


def call(kernel, name, out_shape, operands, flops=0, scratch=(), vmem=8):
    parts = [o if isinstance(o, tuple) else (o,) for o in operands]
    size = sum(p[0].size * p[0].dtype.itemsize for p in parts)
    size += sum(s.size * s.dtype.itemsize for s in out_shape)
    return pl.pallas_call(
        kernel,
        out_shape=out_shape,
        grid=(1,),
        in_specs=[(full, lead, span)[len(p) - 1](*p) for p in parts],
        out_specs=[full(s) for s in out_shape],
        scratch_shapes=scratch,
        compiler_params=pltpu.CompilerParams(vmem_limit_bytes=vmem * 1024 * 1024),
        cost_estimate=pl.CostEstimate(flops=flops, bytes_accessed=size, transcendentals=0),
        name=name,
    )(*[p[0] for p in parts])


def call_loading(kernel, name, out_shape, arrays):
    n = len(arrays)

    def body(*refs):
        sources, outs = refs[:n], refs[n : n + len(out_shape)]
        copies, sems = refs[n + len(out_shape) : -1], refs[-1]
        moves = [
            pltpu.make_async_copy(a, b, sems.at[k])
            for k, (a, b) in enumerate(zip(sources, copies))
        ]
        for m in moves:
            m.start()
        for m in moves:
            m.wait()
        kernel(*copies, *outs)

    return pl.pallas_call(
        body,
        out_shape=out_shape,
        in_specs=[pl.BlockSpec(memory_space=pl.ANY)] * n,
        out_specs=[pl.BlockSpec(memory_space=pltpu.VMEM)] * len(out_shape),
        scratch_shapes=[pltpu.VMEM(a.shape, a.dtype) for a in arrays]
        + [pltpu.SemaphoreType.DMA((n,))],
        compiler_params=pltpu.CompilerParams(vmem_limit_bytes=56 * 1024 * 1024),
        name=name,
    )(*arrays)


def high_low(value):
    high = value.astype(BF).astype(F32)
    return [high, value - high]


def lines_of(lines, width, dtype):
    m = lines[0].shape[1]
    rest = EXTRA - sum(line.shape[0] for line in lines)
    block = jnp.concatenate(lines + [jnp.zeros((rest, m), F32)], axis=0)
    if m < width:
        block = jnp.concatenate([block, jnp.zeros((EXTRA, width - m), F32)], axis=1)
    return block.astype(dtype)


def prepare_kernel(
    routes, slots, combine, tokens, grads, w_in, b_in, w_out, share, raw, places, *outs
):
    units = w_out.shape[1]
    share[0:units] = w_in[0].astype(F32).T.astype(BF)
    share[units : units + EXTRA] = lines_of([b_in[...].astype(F32)], share.shape[1], BF)
    share[units + EXTRA :] = w_out[0]
    n_expert = len(outs)
    cap = outs[0].shape[0]
    n_tok = tokens.shape[0]
    turned = routes[...] - lax.axis_index("x")
    turned = jnp.where(turned < 0, turned + n_expert, turned)
    place = jnp.where(slots[...] < cap, turned * cap + slots[...], -1)
    places[...] = place
    raw[0:n_tok] = grads[...]
    side = [place.astype(F32), combine[...].astype(F32)]
    raw[n_tok:] = lines_of(side, grads.shape[1], BF)
    spots = lax.broadcasted_iota(jnp.int32, (n_expert * cap, n_tok), 0)
    picks = jnp.where((place[0:1, :] == spots) | (place[1:2, :] == spots), 1.0, 0.0)
    rows = dot(picks.astype(BF), tokens[...], NN).astype(BF)
    for s, out in enumerate(outs):
        out[...] = rows[s * cap : (s + 1) * cap]


def douts_kernel(own, below, above, far, *outs):
    cap = outs[0].shape[1]
    n_tok = own.shape[0] - EXTRA
    for z, raw in enumerate((own[...], below[...], above[...], far[...])):
        side = raw[n_tok : n_tok + 4, 0:n_tok].astype(F32)
        spots = lax.broadcasted_iota(jnp.int32, (len(outs) * cap, n_tok), 0)
        place = side[0:2].astype(jnp.int32)
        picks = jnp.where(place[0:1] == spots, side[2:3], 0.0)
        picks = picks + jnp.where(place[1:2] == spots, side[3:4], 0.0)
        rows = dot(picks.astype(BF), raw[0:n_tok], NN).astype(BF)
        for s, out in enumerate(outs):
            out[z] = rows[s * cap : (s + 1) * cap]


def rows_kernel(n_x, n_d, blocks, *refs):
    xs, ds = refs[:n_x], refs[n_x : n_x + n_d]
    mine, below, above, far, other, b_out, *outs = refs[n_x + n_d :]
    x, d, dpre, hidden, *dxs = outs
    shares = [(ours, other.at[k]) for k, ours in enumerate((mine, below, above, far))]
    width = x.shape[1]
    for parts, whole in ((xs, x), (ds, d)):
        at = 0
        for p in parts:
            count = p.shape[-2]
            whole[at : at + count] = p[...].reshape(count, width)
            at += count
    n_y = len(shares)
    unit = (mine.shape[0] - EXTRA) // 2
    xb = x[...]
    db = d[...]

    def w_in_of(k):
        return jnp.concatenate([r[0:unit] for r in shares[k]], axis=0)

    def dots(k):
        bias = jnp.concatenate([r[unit : unit + 1, 0:unit] for r in shares[k]], axis=1)
        w_out = jnp.concatenate([r[unit + EXTRA :] for r in shares[k]], axis=0)
        return dot(xb, w_in_of(k), NT) + bias.astype(F32), dot(db, w_out, NT)

    term = total = grad = None
    now = dots(0)
    for k in range(n_y):
        pre, back = now
        if k + 1 < n_y:
            now = dots(k + 1)
        cdf = 0.5 * (1.0 + lax.erf(pre * 0.7071067811865476))
        dens = jnp.exp(-0.5 * pre * pre) * 0.3989422804014327
        hidden32 = pre * cdf
        new = (back * (cdf + pre * dens)).astype(BF)
        hid = hidden32.astype(BF)
        for c in range(2):
            dpre[c, :, k * unit : (k + 1) * unit] = new[:, c * unit : (c + 1) * unit]
            hidden[c, :, k * unit : (k + 1) * unit] = hid[:, c * unit : (c + 1) * unit]
        by_row = hidden32 * back
        term = by_row if k == 0 else term + by_row
        if k > 0:
            part = dot(grad, w_in_of(k - 1), NN)
            total = part if k == 1 else total + part
        grad = new
    total = total + dot(grad, w_in_of(n_y - 1), NN)
    line = jnp.sum(term.T, axis=0, keepdims=True)
    at = 0
    for (count, is_own), out in zip(blocks, dxs):
        out[0:count] = total[at : at + count].astype(out.dtype)
        here = line[:, at : at + count]
        if is_own:
            by_bias = (d[at : at + count].astype(F32) * b_out[...].astype(F32)).T
            here = here + jnp.sum(by_bias, axis=0, keepdims=True)
            out[count:] = lines_of([here], width, F32)
        else:
            out[count:] = lines_of(high_low(here), width, BF)
        at += count


def rows_set(xs, ds, blocks, w, b_out):
    width = b_out.shape[1]
    m = sum(count for count, _ in blocks)
    units = 4 * (w[0].shape[0] - EXTRA)
    part = jax.ShapeDtypeStruct((2, m, units // 2), BF)
    dxs = [shape(count + EXTRA, width, F32 if own else BF) for count, own in blocks]
    return call(
        functools.partial(rows_kernel, len(xs), len(ds), blocks),
        "rows",
        [shape(m, width), shape(m, width), part, part, *dxs],
        [*xs, *ds, *w, b_out],
        flops=6 * m * units * width,
        vmem=26,
    )


def join_kernel(*refs):
    at = 0
    for ref in refs[:-1]:
        refs[-1][at : at + ref.shape[0]] = ref[...]
        at += ref.shape[0]


def stack_kernel(*refs):
    for k, ref in enumerate(refs[:-1]):
        refs[-1][k] = ref[...]


def sums_kernel(x, d, dpre, hidden, out):
    for c in range(2):
        grads = weight_sums(x[...], d[...], dpre[c], hidden[c])
        at = 0
        for g in grads:
            out[c, at : at + g.shape[0]] = g
            at += g.shape[0]


def weight_sums(x, d, dpre, hidden):
    grad_in = dot(dpre, x, TN)
    grad_out = dot(hidden, d, TN)
    line_in = jnp.sum(dpre.astype(F32), axis=0, keepdims=True)
    line_out = jnp.sum(d.astype(F32), axis=0, keepdims=True)
    line_in = jnp.concatenate(
        [line_in, jnp.zeros((1, d.shape[1] - dpre.shape[1]), F32)], axis=1
    )
    return grad_in, grad_out, lines_of([line_in, line_out], d.shape[1], F32)


def away_kernel(near, x, d, dpre, hidden, out):
    grad_in, grad_out, lines = weight_sums(x[...], d[...], dpre[0], hidden[0])
    units = grad_in.shape[0]
    out[0:units] = (near[0, 0:units] + grad_in).astype(BF)
    out[units : 2 * units] = (near[0, units : 2 * units] + grad_out).astype(BF)
    lines = near[0, 2 * units :] + lines
    out[2 * units :] = lines_of(high_low(lines[0:1]) + high_low(lines[1:2]), out.shape[1], BF)


def home_kernel(near, x, d, dpre, hidden, out):
    at = 0
    for g in weight_sums(x[...], d[...], dpre[0], hidden[0]):
        rows = slice(at, at + g.shape[0])
        out[rows] = near[0, rows] + g
        at += g.shape[0]


def merge_kernel(own, got, *outs):
    units = (own.shape[0] - EXTRA) // 2
    width = own.shape[1]
    lines = own[2 * units : 2 * units + 2]
    side = got[2 * units : 2 * units + 4].astype(F32)
    sum_out = lines[1:2] + side[2:3] + side[3:4]
    side = side[0:1] + side[1:2]
    n_y = len(outs)
    unit = units // n_y
    for k, out in enumerate(outs):
        here = k * unit
        line = lines[0:1, here : here + unit] + side[:, here : here + unit]
        line = jnp.concatenate([line, jnp.zeros((1, width - unit), F32)], axis=1)
        for at in (0, unit):
            rows = slice(at, at + unit)
            from_ = slice(n_y * at + here, n_y * at + here + unit)
            total = own[from_] + got[from_].astype(F32)
            out[rows] = total.astype(out.dtype)
        if k == 0:
            both = [line, jnp.zeros_like(line), sum_out]
        else:
            both = high_low(line) + high_low(sum_out)
        out[2 * unit :] = lines_of(both, width, out.dtype)


def last_kernel(own, a, b, c, grad_in, grad_bias_in, grad_out, grad_bias_out):
    units = grad_out.shape[1]
    total = own[...] + a[...].astype(F32) + b[...].astype(F32) + c[...].astype(F32)
    grad_in[0] = total[0:units].T.astype(BF)
    grad_out[0] = total[units : 2 * units].astype(BF)
    tail = total[2 * units :]
    grad_bias_in[...] = (tail[0:1] + tail[1:2])[:, 0:units]
    grad_bias_out[...] = tail[2:3] + tail[3:4]


ORDER = (0, 1, 3, 2)


def sum_kernel(n_early, *refs):
    early, late, (far, out) = refs[:3], refs[3:6], refs[6:]
    n_expert = out.shape[0]
    here = lax.axis_index("x")
    width = far.shape[1]
    m = far.shape[0] - EXTRA
    cap = m // n_expert
    e = sum(r[...].astype(F32) for r in early)
    t = sum(r[...].astype(F32) for r in late)
    cut = n_early * cap
    line = [v[n : n + 1, 0:n] + v[n + 1 : n + 2, 0:n] for v, n in ((e, cut), (t, m - cut))]
    side = far[m : m + 2].astype(F32)
    line = jnp.concatenate(line, axis=1) + side[0:1, 0:m] + side[1:2, 0:m]
    lines = lines_of(high_low(line), width, BF)
    for k, s in enumerate(ORDER):
        to = lax.rem(here + (n_expert - s), n_expert)
        rows = slice(k * cap, (k + 1) * cap)
        total = e[rows] if k < n_early else t[k * cap - cut : (k + 1) * cap - cut]
        out[to, 0:cap] = (total + far[rows].astype(F32)).astype(BF)
        out[to, cap:] = lines


def finish_kernel(places, weights, pieces, out, by_weight):
    n_expert = pieces.shape[0]
    cap = pieces.shape[1] - EXTRA
    n_tok = places.shape[1]
    here = lax.axis_index("x")
    total = None
    sums = [None, None]
    spots = lax.broadcasted_iota(jnp.int32, (n_expert * cap, n_tok), 0)
    picks = [jnp.where(places[k : k + 1, :] == spots, 1.0, 0.0) for k in range(2)]
    both = (picks[0] + picks[1]).astype(BF)
    for s in range(n_expert):
        piece = pieces.at[lax.rem(here + s, n_expert)]
        part = dot(both[s * cap : (s + 1) * cap], piece[0:cap], TN)
        total = part if total is None else total + part
        lane = spots - ORDER.index(s) * cap
        inside = (lane >= 0) & (lane < cap)
        for k in range(2):
            pick = inside & (places[k : k + 1, :] == lane + s * cap)
            pick = jnp.where(pick, 1.0, 0.0).astype(BF)
            found = dot(piece[cap:, 0 : n_expert * cap], pick, NN)
            line = found[0:1] + found[1:2]
            sums[k] = line if sums[k] is None else sums[k] + line
    out[...] = total.astype(BF)
    by_weight[...] = jnp.concatenate(sums, axis=0) / weights[...].astype(F32)


def on_device(tokens, grads_out, routes, slots, combine, w_in, b_in, w_out, b_out):
    n_expert = lax.axis_size("x")
    tok_rows, width = tokens.shape
    cap = 2 * tok_rows // n_expert
    units = w_in.shape[2]

    barrier = lax.optimization_barrier

    mine, raw, places, *x_sent = call_loading(
        prepare_kernel,
        "prepare",
        [
            shape(2 * units + EXTRA, width),
            shape(tok_rows + EXTRA, width),
            shape(2, tok_rows, jnp.int32),
        ]
        + [shape(cap, width)] * n_expert,
        [routes.T, slots.T, combine.T, tokens, grads_out, w_in, b_in, w_out],
    )
    raw_below = shift(raw, "z", 1)
    raw_above = shift(raw, "z", -1)
    x_1 = shift(x_sent[1], "x", 1)
    x_3 = shift(x_sent[3], "x", -1)
    w_below = shift(mine, "y", 1)
    w_above = shift(mine, "y", -1)
    raw_below, raw_above, x_1, x_2, x_3 = barrier((raw_below, raw_above, x_1, x_sent[2], x_3))
    raw_far = shift(raw_below, "z", 1)
    x_own = [x_sent[0], x_1, x_3, shift(x_2, "x", 2)]
    x_own = call(join_kernel, "join", [shape(n_expert * cap, width)], x_own)[0]
    x_own, raw_far, w_below, w_above = barrier((x_own, raw_far, w_below, w_above))

    d_sent = call(
        douts_kernel,
        "douts",
        [jax.ShapeDtypeStruct((4, cap, width), BF)] * n_expert,
        [raw, raw_below, raw_above, raw_far],
    )
    x_below = shift(x_own, "z", 1)
    x_above = shift(x_own, "z", -1)
    w_far = shift(w_below, "y", 1)
    d_1 = shift(d_sent[1], "x", 1)
    d_3 = shift(d_sent[3], "x", -1)
    x_below, x_above, w_far, d_1, d_3, d_2 = barrier(
        (x_below, x_above, w_far, d_1, d_3, d_sent[2])
    )
    ours = [mine, w_below, w_above, w_far]
    every = call(stack_kernel, "stack", [jax.ShapeDtypeStruct((4, *mine.shape), BF)], ours, vmem=12)
    w = [*ours, shift(every[0], "c", 1)]

    d_2 = shift(d_2, "x", 2)
    half = x_own.shape[0] // 2
    x_far_a = shift(x_below[:half], "z", 1)
    x_far_b = shift(x_above[half:], "z", -1)
    n_early = 3
    cut = n_early * cap
    sides = (x_own, x_below, x_above)
    early = rows_set(
        [(a, 0, cut) for a in sides],
        [(a, z) for z in range(3) for a in (d_sent[0], d_1, d_3)],
        [(cut, True), (cut, False), (cut, False)],
        w,
        b_out,
    )
    acc = call(
        sums_kernel,
        "sums",
        [jax.ShapeDtypeStruct((2, 8 * units + EXTRA, width), F32)],
        early[:4],
        flops=8 * 3 * cut * 4 * units * width,
        vmem=28,
    )[0]
    early_above = shift(early[6], "z", 1)
    early_below = shift(early[5], "z", -1)
    d_2, x_far_a, x_far_b, acc = barrier((d_2, x_far_a, x_far_b, acc))
    late = rows_set(
        [(a, cut, cap) for a in sides] + [x_far_a, x_far_b],
        [(d_2, z) for z in range(3)] + [(a, 3) for a in (d_sent[0], d_1, d_3, d_2)],
        [(cap, True), (cap, False), (cap, False), (n_expert * cap, False)],
        w,
        b_out,
    )

    ends = [late[0], late[1], late[2], late[3]]
    flops = 4 * 7 * cap * 4 * units * width
    out = shape(8 * units + EXTRA, width)
    operands = [(acc, 1), *ends[:2], (late[2], 1), (late[3], 1)]
    away = call(away_kernel, "away", [out], operands, flops, vmem=20)[0]
    away, early_above, early_below = barrier((away, early_above, early_below))
    got = shift(away, "c", 1)
    out = shape(8 * units + EXTRA, width, F32)
    operands = [(acc, 0), *ends[:2], (late[2], 0), (late[3], 0)]
    home = call(home_kernel, "home", [out], operands, flops, vmem=24)[0]
    home = call(
        merge_kernel,
        "merge",
        [shape(2 * units + EXTRA, width, BF if k else F32) for k in range(4)],
        [home, got],
        vmem=16,
    )

    far = shift(late[7], "z", 2)
    late_above = shift(late[6], "z", 1)
    late_below = shift(late[5], "z", -1)
    pieces = call(
        functools.partial(sum_kernel, n_early),
        "sum_z",
        [jax.ShapeDtypeStruct((n_expert, cap + EXTRA, width), BF)],
        [early[4], early_above, early_below, late[4], late_above, late_below, far],
    )[0]
    final = lax.all_to_all(pieces, "x", 0, 0, tiled=True)
    moved = [shift(home[k], "y", step) for k, step in ((3, 2), (1, -1), (2, 1))]
    grad_tokens, by_weight = call(
        finish_kernel,
        "finish",
        [shape(tok_rows, width), shape(2, tok_rows, F32)],
        [places, combine.T, final],
    )
    grad_w_in, grad_b_in, grad_w_out, grad_b_out = call(
        last_kernel,
        "last",
        [
            jax.ShapeDtypeStruct(w_in.shape, BF),
            shape(1, units, F32),
            jax.ShapeDtypeStruct(w_out.shape, BF),
            shape(1, width, F32),
        ],
        [home[0], *moved],
    )
    return (grad_tokens, by_weight.T, grad_w_in, grad_b_in, grad_w_out, grad_b_out)


def solution(mesh):
    fine = Mesh(mesh.devices.reshape(4, 4, 4, 2), ("x", "z", "y", "c"))
    zero = ("z", "y", "c")
    rows = P(("x", "z", "y", "c"), None)
    in_specs = (rows,) * 5 + (
        P("x", None, zero),
        P("x", zero),
        P("x", zero, None),
        P("x", None),
    )
    out_specs = (rows, rows) + in_specs[5:]
    return jax.shard_map(
        on_device, mesh=fine, in_specs=in_specs, out_specs=out_specs, check_vma=False
    )
```

```python
import functools

import jax
import jax.numpy as jnp
from jax import lax
from jax.experimental import pallas as pl
from jax.experimental.pallas import tpu as pltpu
from jax.sharding import Mesh, PartitionSpec as P

BF = jnp.bfloat16
F32 = jnp.float32
EXTRA = 16
NT = (((1,), (1,)), ((), ()))
NN = (((1,), (0,)), ((), ()))
TN = (((0,), (0,)), ((), ()))


def dot(a, b, dims):
    return lax.dot_general(a, b, dims, preferred_element_type=F32)


def shift(value, axis, step):
    n = lax.axis_size(axis)
    return lax.ppermute(value, axis, [(i, (i + step) % n) for i in range(n)])


def shape(rows, columns, dtype=BF):
    return jax.ShapeDtypeStruct((rows, columns), dtype)


def full(a):
    return pl.BlockSpec(a.shape, lambda i: (0,) * len(a.shape))


def span(a, first, rows):
    return pl.BlockSpec((rows, a.shape[1]), lambda i: (first // rows, 0))


def lead(a, index):
    return pl.BlockSpec((1, *a.shape[1:]), lambda i: (index,) + (0,) * (len(a.shape) - 1))


def call(kernel, name, out_shape, operands, flops=0, scratch=(), vmem=8):
    parts = [o if isinstance(o, tuple) else (o,) for o in operands]
    size = sum(p[0].size * p[0].dtype.itemsize for p in parts)
    size += sum(s.size * s.dtype.itemsize for s in out_shape)
    return pl.pallas_call(
        kernel,
        out_shape=out_shape,
        grid=(1,),
        in_specs=[(full, lead, span)[len(p) - 1](*p) for p in parts],
        out_specs=[full(s) for s in out_shape],
        scratch_shapes=scratch,
        compiler_params=pltpu.CompilerParams(vmem_limit_bytes=vmem * 1024 * 1024),
        cost_estimate=pl.CostEstimate(flops=flops, bytes_accessed=size, transcendentals=0),
        name=name,
    )(*[p[0] for p in parts])


def call_loading(kernel, name, out_shape, arrays):
    n = len(arrays)

    def body(*refs):
        sources, outs = refs[:n], refs[n : n + len(out_shape)]
        copies, sems = refs[n + len(out_shape) : -1], refs[-1]
        moves = [
            pltpu.make_async_copy(a, b, sems.at[k])
            for k, (a, b) in enumerate(zip(sources, copies))
        ]
        for m in moves:
            m.start()
        for m in moves:
            m.wait()
        kernel(*copies, *outs)

    return pl.pallas_call(
        body,
        out_shape=out_shape,
        in_specs=[pl.BlockSpec(memory_space=pl.ANY)] * n,
        out_specs=[pl.BlockSpec(memory_space=pltpu.VMEM)] * len(out_shape),
        scratch_shapes=[pltpu.VMEM(a.shape, a.dtype) for a in arrays]
        + [pltpu.SemaphoreType.DMA((n,))],
        compiler_params=pltpu.CompilerParams(vmem_limit_bytes=56 * 1024 * 1024),
        name=name,
    )(*arrays)


def high_low(value):
    high = value.astype(BF).astype(F32)
    return [high, value - high]


def lines_of(lines, width, dtype):
    m = lines[0].shape[1]
    rest = EXTRA - sum(line.shape[0] for line in lines)
    block = jnp.concatenate(lines + [jnp.zeros((rest, m), F32)], axis=0)
    if m < width:
        block = jnp.concatenate([block, jnp.zeros((EXTRA, width - m), F32)], axis=1)
    return block.astype(dtype)


def prepare_kernel(
    routes, slots, combine, tokens, grads, w_in, b_in, w_out, share, raw, places, *outs
):
    units = w_out.shape[1]
    share[0:units] = w_in[0].astype(F32).T.astype(BF)
    share[units : units + EXTRA] = lines_of([b_in[...].astype(F32)], share.shape[1], BF)
    share[units + EXTRA :] = w_out[0]
    n_expert = len(outs)
    cap = outs[0].shape[1]
    n_tok = tokens.shape[0]
    turned = routes[...] - lax.axis_index("x")
    turned = jnp.where(turned < 0, turned + n_expert, turned)
    place = jnp.where(slots[...] < cap, turned * cap + slots[...], -1)
    places[...] = place
    raw[0:n_tok] = grads[...]
    side = [place.astype(F32), combine[...].astype(F32)]
    raw[n_tok:] = lines_of(side, grads.shape[1], BF)
    spots = lax.broadcasted_iota(jnp.int32, (n_expert * cap, n_tok), 0)
    first, second = place[0:1] == spots, place[1:2] == spots
    picks = jnp.where(first | second, 1.0, 0.0)
    weights = combine[...].astype(F32)
    scaled = jnp.where(first, weights[0:1], 0.0) + jnp.where(second, weights[1:2], 0.0)
    rows_x = dot(picks.astype(BF), tokens[...], NN).astype(BF)
    rows_d = dot(scaled.astype(BF), grads[...], NN).astype(BF)
    for s, out in enumerate(outs):
        out[0] = rows_x[s * cap : (s + 1) * cap]
        out[1] = rows_d[s * cap : (s + 1) * cap]


def douts_kernel(below, above, far, *outs):
    cap = outs[0].shape[1]
    n_tok = below.shape[0] - EXTRA
    for z, raw in enumerate((below[...], above[...], far[...])):
        side = raw[n_tok : n_tok + 4, 0:n_tok].astype(F32)
        spots = lax.broadcasted_iota(jnp.int32, (len(outs) * cap, n_tok), 0)
        place = side[0:2].astype(jnp.int32)
        picks = jnp.where(place[0:1] == spots, side[2:3], 0.0)
        picks = picks + jnp.where(place[1:2] == spots, side[3:4], 0.0)
        rows = dot(picks.astype(BF), raw[0:n_tok], NN).astype(BF)
        for s, out in enumerate(outs):
            out[z] = rows[s * cap : (s + 1) * cap]


def rows_kernel(n_x, n_d, blocks, *refs):
    xs, ds = refs[:n_x], refs[n_x : n_x + n_d]
    mine, below, above, far, other, b_out, *outs = refs[n_x + n_d :]
    x, d, dpre, hidden, *dxs = outs
    shares = [(ours, other.at[k]) for k, ours in enumerate((mine, below, above, far))]
    width = x.shape[1]
    for parts, whole in ((xs, x), (ds, d)):
        at = 0
        for p in parts:
            count = p.shape[-2]
            whole[at : at + count] = p[...].reshape(count, width)
            at += count
    n_y = len(shares)
    unit = (mine.shape[0] - EXTRA) // 2
    xb = x[...]
    db = d[...]

    def w_in_of(k):
        return jnp.concatenate([r[0:unit] for r in shares[k]], axis=0)

    def dots(k):
        bias = jnp.concatenate([r[unit : unit + 1, 0:unit] for r in shares[k]], axis=1)
        w_out = jnp.concatenate([r[unit + EXTRA :] for r in shares[k]], axis=0)
        return dot(xb, w_in_of(k), NT) + bias.astype(F32), dot(db, w_out, NT)

    term = total = grad = None
    now = dots(0)
    for k in range(n_y):
        pre, back = now
        if k + 1 < n_y:
            now = dots(k + 1)
        cdf = 0.5 * (1.0 + lax.erf(pre * 0.7071067811865476))
        dens = jnp.exp(-0.5 * pre * pre) * 0.3989422804014327
        hidden32 = pre * cdf
        new = (back * (cdf + pre * dens)).astype(BF)
        hid = hidden32.astype(BF)
        for c in range(2):
            dpre[c, :, k * unit : (k + 1) * unit] = new[:, c * unit : (c + 1) * unit]
            hidden[c, :, k * unit : (k + 1) * unit] = hid[:, c * unit : (c + 1) * unit]
        by_row = hidden32 * back
        term = by_row if k == 0 else term + by_row
        if k > 0:
            part = dot(grad, w_in_of(k - 1), NN)
            total = part if k == 1 else total + part
        grad = new
    total = total + dot(grad, w_in_of(n_y - 1), NN)
    line = jnp.sum(term.T, axis=0, keepdims=True)
    at = 0
    for (count, is_own), out in zip(blocks, dxs):
        out[0:count] = total[at : at + count].astype(out.dtype)
        here = line[:, at : at + count]
        if is_own:
            by_bias = (d[at : at + count].astype(F32) * b_out[...].astype(F32)).T
            here = here + jnp.sum(by_bias, axis=0, keepdims=True)
            out[count:] = lines_of([here], width, F32)
        else:
            out[count:] = lines_of(high_low(here), width, BF)
        at += count


def rows_set(xs, ds, blocks, w, b_out):
    width = b_out.shape[1]
    m = sum(count for count, _ in blocks)
    units = 4 * (w[0].shape[0] - EXTRA)
    part = jax.ShapeDtypeStruct((2, m, units // 2), BF)
    dxs = [shape(count + EXTRA, width, F32 if own else BF) for count, own in blocks]
    return call(
        functools.partial(rows_kernel, len(xs), len(ds), blocks),
        "rows",
        [shape(m, width), shape(m, width), part, part, *dxs],
        [*xs, *ds, *w, b_out],
        flops=6 * m * units * width,
        vmem=26,
    )


def join_kernel(*refs):
    cap = refs[0].shape[1]
    for k, ref in enumerate(refs[:-1]):
        refs[-1][k * cap : (k + 1) * cap] = ref[0]


def stack_kernel(*refs):
    for k, ref in enumerate(refs[:-1]):
        refs[-1][k] = ref[...]


def sums_kernel(x, d, dpre, hidden, out):
    for c in range(2):
        grads = weight_sums(x[...], d[...], dpre[c], hidden[c])
        at = 0
        for g in grads:
            out[c, at : at + g.shape[0]] = g
            at += g.shape[0]


def weight_sums(x, d, dpre, hidden):
    grad_in = dot(dpre, x, TN)
    grad_out = dot(hidden, d, TN)
    line_in = jnp.sum(dpre.astype(F32), axis=0, keepdims=True)
    line_out = jnp.sum(d.astype(F32), axis=0, keepdims=True)
    line_in = jnp.concatenate(
        [line_in, jnp.zeros((1, d.shape[1] - dpre.shape[1]), F32)], axis=1
    )
    return grad_in, grad_out, lines_of([line_in, line_out], d.shape[1], F32)


def away_kernel(near, x, d, dpre, hidden, out):
    grad_in, grad_out, lines = weight_sums(x[...], d[...], dpre[0], hidden[0])
    units = grad_in.shape[0]
    out[0:units] = (near[0, 0:units] + grad_in).astype(BF)
    out[units : 2 * units] = (near[0, units : 2 * units] + grad_out).astype(BF)
    lines = near[0, 2 * units :] + lines
    out[2 * units :] = lines_of(high_low(lines[0:1]) + high_low(lines[1:2]), out.shape[1], BF)


def home_kernel(near, x, d, dpre, hidden, out):
    at = 0
    for g in weight_sums(x[...], d[...], dpre[0], hidden[0]):
        rows = slice(at, at + g.shape[0])
        out[rows] = near[0, rows] + g
        at += g.shape[0]


def merge_kernel(own, got, *outs):
    units = (own.shape[0] - EXTRA) // 2
    width = own.shape[1]
    lines = own[2 * units : 2 * units + 2]
    side = got[2 * units : 2 * units + 4].astype(F32)
    sum_out = lines[1:2] + side[2:3] + side[3:4]
    side = side[0:1] + side[1:2]
    n_y = len(outs)
    unit = units // n_y
    for k, out in enumerate(outs):
        here = k * unit
        line = lines[0:1, here : here + unit] + side[:, here : here + unit]
        line = jnp.concatenate([line, jnp.zeros((1, width - unit), F32)], axis=1)
        for at in (0, unit):
            rows = slice(at, at + unit)
            from_ = slice(n_y * at + here, n_y * at + here + unit)
            total = own[from_] + got[from_].astype(F32)
            out[rows] = total.astype(out.dtype)
        if k == 0:
            both = [line, jnp.zeros_like(line), sum_out]
        else:
            both = high_low(line) + high_low(sum_out)
        out[2 * unit :] = lines_of(both, width, out.dtype)


def last_kernel(own, a, b, c, grad_in, grad_bias_in, grad_out, grad_bias_out):
    units = grad_out.shape[1]
    total = own[...] + a[...].astype(F32) + b[...].astype(F32) + c[...].astype(F32)
    grad_in[0] = total[0:units].T.astype(BF)
    grad_out[0] = total[units : 2 * units].astype(BF)
    tail = total[2 * units :]
    grad_bias_in[...] = (tail[0:1] + tail[1:2])[:, 0:units]
    grad_bias_out[...] = tail[2:3] + tail[3:4]


ORDER = (0, 1, 3, 2)


def sum_kernel(n_early, *refs):
    early, late, (far, out) = refs[:3], refs[3:6], refs[6:]
    n_expert = out.shape[0]
    here = lax.axis_index("x")
    width = far.shape[1]
    m = far.shape[0] - EXTRA
    cap = m // n_expert
    e = sum(r[...].astype(F32) for r in early)
    t = sum(r[...].astype(F32) for r in late)
    cut = n_early * cap
    line = [v[n : n + 1, 0:n] + v[n + 1 : n + 2, 0:n] for v, n in ((e, cut), (t, m - cut))]
    side = far[m : m + 2].astype(F32)
    line = jnp.concatenate(line, axis=1) + side[0:1, 0:m] + side[1:2, 0:m]
    lines = lines_of(high_low(line), width, BF)
    for k, s in enumerate(ORDER):
        to = lax.rem(here + (n_expert - s), n_expert)
        rows = slice(k * cap, (k + 1) * cap)
        total = e[rows] if k < n_early else t[k * cap - cut : (k + 1) * cap - cut]
        out[to, 0:cap] = (total + far[rows].astype(F32)).astype(BF)
        out[to, cap:] = lines


def finish_kernel(places, weights, pieces, out, by_weight):
    n_expert = pieces.shape[0]
    cap = pieces.shape[1] - EXTRA
    n_tok = places.shape[1]
    here = lax.axis_index("x")
    total = None
    sums = [None, None]
    spots = lax.broadcasted_iota(jnp.int32, (n_expert * cap, n_tok), 0)
    picks = [jnp.where(places[k : k + 1, :] == spots, 1.0, 0.0) for k in range(2)]
    both = (picks[0] + picks[1]).astype(BF)
    for s in range(n_expert):
        piece = pieces.at[lax.rem(here + s, n_expert)]
        part = dot(both[s * cap : (s + 1) * cap], piece[0:cap], TN)
        total = part if total is None else total + part
        lane = spots - ORDER.index(s) * cap
        inside = (lane >= 0) & (lane < cap)
        for k in range(2):
            pick = inside & (places[k : k + 1, :] == lane + s * cap)
            pick = jnp.where(pick, 1.0, 0.0).astype(BF)
            found = dot(piece[cap:, 0 : n_expert * cap], pick, NN)
            line = found[0:1] + found[1:2]
            sums[k] = line if sums[k] is None else sums[k] + line
    out[...] = total.astype(BF)
    by_weight[...] = jnp.concatenate(sums, axis=0) / weights[...].astype(F32)


def on_device(tokens, grads_out, routes, slots, combine, w_in, b_in, w_out, b_out):
    n_expert = lax.axis_size("x")
    tok_rows, width = tokens.shape
    cap = 2 * tok_rows // n_expert
    units = w_in.shape[2]

    barrier = lax.optimization_barrier

    mine, raw, places, *x_sent = call_loading(
        prepare_kernel,
        "prepare",
        [
            shape(2 * units + EXTRA, width),
            shape(tok_rows + EXTRA, width),
            shape(2, tok_rows, jnp.int32),
        ]
        + [jax.ShapeDtypeStruct((2, cap, width), BF)] * n_expert,
        [routes.T, slots.T, combine.T, tokens, grads_out, w_in, b_in, w_out],
    )
    raw_below = shift(raw, "z", 1)
    raw_above = shift(raw, "z", -1)
    x_1 = shift(x_sent[1], "x", 1)
    x_3 = shift(x_sent[3], "x", -1)
    w_below = shift(mine, "y", 1)
    w_above = shift(mine, "y", -1)
    raw_below, raw_above, x_1, x_2, x_3 = barrier((raw_below, raw_above, x_1, x_sent[2], x_3))
    raw_far = shift(raw_below, "z", 1)
    x_2 = shift(x_2, "x", 2)
    x_got = [x_sent[0], x_1, x_3, x_2]
    x_own = call(join_kernel, "join", [shape(n_expert * cap, width)], x_got)[0]
    x_own, raw_far, w_below, w_above = barrier((x_own, raw_far, w_below, w_above))

    d_sent = call(
        douts_kernel,
        "douts",
        [jax.ShapeDtypeStruct((3, cap, width), BF)] * n_expert,
        [raw_below, raw_above, raw_far],
    )
    x_below = shift(x_own, "z", 1)
    x_above = shift(x_own, "z", -1)
    w_far = shift(w_below, "y", 1)
    d_1 = shift(d_sent[1], "x", 1)
    d_3 = shift(d_sent[3], "x", -1)
    x_below, x_above, w_far, d_1, d_3, d_2 = barrier(
        (x_below, x_above, w_far, d_1, d_3, d_sent[2])
    )
    ours = [mine, w_below, w_above, w_far]
    every = call(stack_kernel, "stack", [jax.ShapeDtypeStruct((4, *mine.shape), BF)], ours, vmem=12)
    w = [*ours, shift(every[0], "c", 1)]

    d_2 = shift(d_2, "x", 2)
    half = x_own.shape[0] // 2
    x_far_a = shift(x_below[:half], "z", 1)
    x_far_b = shift(x_above[half:], "z", -1)
    n_early = 3
    cut = n_early * cap
    sides = (x_own, x_below, x_above)
    early = rows_set(
        [(a, 0, cut) for a in sides],
        [(a, 1) for a in x_got[:3]] + [(a, z) for z in range(2) for a in (d_sent[0], d_1, d_3)],
        [(cut, True), (cut, False), (cut, False)],
        w,
        b_out,
    )
    acc = call(
        sums_kernel,
        "sums",
        [jax.ShapeDtypeStruct((2, 8 * units + EXTRA, width), F32)],
        early[:4],
        flops=8 * 3 * cut * 4 * units * width,
        vmem=28,
    )[0]
    early_above = shift(early[6], "z", 1)
    early_below = shift(early[5], "z", -1)
    d_2, x_far_a, x_far_b, acc = barrier((d_2, x_far_a, x_far_b, acc))
    late = rows_set(
        [(a, cut, cap) for a in sides] + [x_far_a, x_far_b],
        [(x_2, 1), (d_2, 0), (d_2, 1)] + [(a, 2) for a in (d_sent[0], d_1, d_3, d_2)],
        [(cap, True), (cap, False), (cap, False), (n_expert * cap, False)],
        w,
        b_out,
    )

    ends = [late[0], late[1], late[2], late[3]]
    flops = 4 * 7 * cap * 4 * units * width
    out = shape(8 * units + EXTRA, width)
    operands = [(acc, 1), *ends[:2], (late[2], 1), (late[3], 1)]
    away = call(away_kernel, "away", [out], operands, flops, vmem=20)[0]
    away, early_above, early_below = barrier((away, early_above, early_below))
    got = shift(away, "c", 1)
    out = shape(8 * units + EXTRA, width, F32)
    operands = [(acc, 0), *ends[:2], (late[2], 0), (late[3], 0)]
    home = call(home_kernel, "home", [out], operands, flops, vmem=24)[0]
    home = call(
        merge_kernel,
        "merge",
        [shape(2 * units + EXTRA, width, BF if k else F32) for k in range(4)],
        [home, got],
        vmem=16,
    )

    far = shift(late[7], "z", 2)
    late_above = shift(late[6], "z", 1)
    late_below = shift(late[5], "z", -1)
    pieces = call(
        functools.partial(sum_kernel, n_early),
        "sum_z",
        [jax.ShapeDtypeStruct((n_expert, cap + EXTRA, width), BF)],
        [early[4], early_above, early_below, late[4], late_above, late_below, far],
    )[0]
    final = lax.all_to_all(pieces, "x", 0, 0, tiled=True)
    moved = [shift(home[k], "y", step) for k, step in ((3, 2), (1, -1), (2, 1))]
    grad_tokens, by_weight = call(
        finish_kernel,
        "finish",
        [shape(tok_rows, width), shape(2, tok_rows, F32)],
        [places, combine.T, final],
    )
    grad_w_in, grad_b_in, grad_w_out, grad_b_out = call(
        last_kernel,
        "last",
        [
            jax.ShapeDtypeStruct(w_in.shape, BF),
            shape(1, units, F32),
            jax.ShapeDtypeStruct(w_out.shape, BF),
            shape(1, width, F32),
        ],
        [home[0], *moved],
    )
    return (grad_tokens, by_weight.T, grad_w_in, grad_b_in, grad_w_out, grad_b_out)


def solution(mesh):
    fine = Mesh(mesh.devices.reshape(4, 4, 4, 2), ("x", "z", "y", "c"))
    zero = ("z", "y", "c")
    rows = P(("x", "z", "y", "c"), None)
    in_specs = (rows,) * 5 + (
        P("x", None, zero),
        P("x", zero),
        P("x", zero, None),
        P("x", None),
    )
    out_specs = (rows, rows) + in_specs[5:]
    return jax.shard_map(
        on_device, mesh=fine, in_specs=in_specs, out_specs=out_specs, check_vma=False
    )
```

```python
import functools

import jax
import jax.numpy as jnp
from jax import lax
from jax.experimental import pallas as pl
from jax.experimental.pallas import tpu as pltpu
from jax.sharding import Mesh, PartitionSpec as P

BF = jnp.bfloat16
F32 = jnp.float32
EXTRA = 16
NT = (((1,), (1,)), ((), ()))
NN = (((1,), (0,)), ((), ()))
TN = (((0,), (0,)), ((), ()))


def dot(a, b, dims):
    return lax.dot_general(a, b, dims, preferred_element_type=F32)


def shift(value, axis, step):
    n = lax.axis_size(axis)
    return lax.ppermute(value, axis, [(i, (i + step) % n) for i in range(n)])


def shape(rows, columns, dtype=BF):
    return jax.ShapeDtypeStruct((rows, columns), dtype)


def full(a):
    return pl.BlockSpec(a.shape, lambda i: (0,) * len(a.shape))


def span(a, first, rows):
    return pl.BlockSpec((rows, a.shape[1]), lambda i: (first // rows, 0))


def lead(a, index):
    return pl.BlockSpec((1, *a.shape[1:]), lambda i: (index,) + (0,) * (len(a.shape) - 1))


def call(kernel, name, out_shape, operands, flops=0, scratch=(), vmem=8):
    parts = [o if isinstance(o, tuple) else (o,) for o in operands]
    size = sum(p[0].size * p[0].dtype.itemsize for p in parts)
    size += sum(s.size * s.dtype.itemsize for s in out_shape)
    return pl.pallas_call(
        kernel,
        out_shape=out_shape,
        grid=(1,),
        in_specs=[(full, lead, span)[len(p) - 1](*p) for p in parts],
        out_specs=[full(s) for s in out_shape],
        scratch_shapes=scratch,
        compiler_params=pltpu.CompilerParams(vmem_limit_bytes=vmem * 1024 * 1024),
        cost_estimate=pl.CostEstimate(flops=flops, bytes_accessed=size, transcendentals=0),
        name=name,
    )(*[p[0] for p in parts])


def call_loading(kernel, name, out_shape, arrays):
    n = len(arrays)

    def body(*refs):
        sources, outs = refs[:n], refs[n : n + len(out_shape)]
        copies, sems = refs[n + len(out_shape) : -1], refs[-1]
        moves = [
            pltpu.make_async_copy(a, b, sems.at[k])
            for k, (a, b) in enumerate(zip(sources, copies))
        ]
        for m in moves:
            m.start()
        for m in moves:
            m.wait()
        kernel(*copies, *outs)

    return pl.pallas_call(
        body,
        out_shape=out_shape,
        in_specs=[pl.BlockSpec(memory_space=pl.ANY)] * n,
        out_specs=[pl.BlockSpec(memory_space=pltpu.VMEM)] * len(out_shape),
        scratch_shapes=[pltpu.VMEM(a.shape, a.dtype) for a in arrays]
        + [pltpu.SemaphoreType.DMA((n,))],
        compiler_params=pltpu.CompilerParams(vmem_limit_bytes=56 * 1024 * 1024),
        name=name,
    )(*arrays)


def high_low(value):
    high = value.astype(BF).astype(F32)
    return [high, value - high]


def lines_of(lines, width, dtype):
    m = lines[0].shape[1]
    rest = EXTRA - sum(line.shape[0] for line in lines)
    block = jnp.concatenate(lines + [jnp.zeros((rest, m), F32)], axis=0)
    if m < width:
        block = jnp.concatenate([block, jnp.zeros((EXTRA, width - m), F32)], axis=1)
    return block.astype(dtype)


def prepare_kernel(
    routes, slots, combine, tokens, grads, w_in, b_in, w_out, share, raw, places, *outs
):
    units = w_out.shape[1]
    share[0:units] = w_in[0].T
    share[units : units + EXTRA] = lines_of([b_in[...].astype(F32)], share.shape[1], BF)
    share[units + EXTRA :] = w_out[0]
    n_expert = len(outs)
    cap = outs[0].shape[1]
    n_tok = tokens.shape[0]
    turned = routes[...] - lax.axis_index("x")
    turned = jnp.where(turned < 0, turned + n_expert, turned)
    place = jnp.where(slots[...] < cap, turned * cap + slots[...], -1)
    places[...] = place
    raw[0:n_tok] = grads[...]
    side = [place.astype(F32), combine[...].astype(F32)]
    raw[n_tok:] = lines_of(side, grads.shape[1], BF)
    spots = lax.broadcasted_iota(jnp.int32, (n_expert * cap, n_tok), 0)
    first, second = place[0:1] == spots, place[1:2] == spots
    picks = jnp.where(first | second, 1.0, 0.0)
    weights = combine[...].astype(F32)
    scaled = jnp.where(first, weights[0:1], 0.0) + jnp.where(second, weights[1:2], 0.0)
    rows_x = dot(picks.astype(BF), tokens[...], NN).astype(BF)
    rows_d = dot(scaled.astype(BF), grads[...], NN).astype(BF)
    for s, out in enumerate(outs):
        out[0] = rows_x[s * cap : (s + 1) * cap]
        out[1] = rows_d[s * cap : (s + 1) * cap]


def douts_kernel(below, above, far, *outs):
    cap = outs[0].shape[1]
    n_tok = below.shape[0] - EXTRA
    for z, raw in enumerate((below[...], above[...], far[...])):
        side = raw[n_tok : n_tok + 4, 0:n_tok].astype(F32)
        spots = lax.broadcasted_iota(jnp.int32, (len(outs) * cap, n_tok), 0)
        place = side[0:2].astype(jnp.int32)
        picks = jnp.where(place[0:1] == spots, side[2:3], 0.0)
        picks = picks + jnp.where(place[1:2] == spots, side[3:4], 0.0)
        rows = dot(picks.astype(BF), raw[0:n_tok], NN).astype(BF)
        for s, out in enumerate(outs):
            out[z] = rows[s * cap : (s + 1) * cap]


def rows_kernel(n_x, n_d, blocks, *refs):
    xs, ds = refs[:n_x], refs[n_x : n_x + n_d]
    mine, below, above, far, other, b_out, *outs = refs[n_x + n_d :]
    x, d, dpre, hidden, *dxs = outs
    shares = [(ours, other.at[k]) for k, ours in enumerate((mine, below, above, far))]
    width = x.shape[1]
    for parts, whole in ((xs, x), (ds, d)):
        at = 0
        for p in parts:
            count = p.shape[-2]
            whole[at : at + count] = p[...].reshape(count, width)
            at += count
    n_y = len(shares)
    unit = (mine.shape[0] - EXTRA) // 2
    xb = x[...]
    db = d[...]

    def w_in_of(k):
        return jnp.concatenate([r[0:unit] for r in shares[k]], axis=0)

    def dots(k):
        bias = jnp.concatenate([r[unit : unit + 1, 0:unit] for r in shares[k]], axis=1)
        w_out = jnp.concatenate([r[unit + EXTRA :] for r in shares[k]], axis=0)
        return dot(xb, w_in_of(k), NT) + bias.astype(F32), dot(db, w_out, NT)

    term = total = grad = None
    now = dots(0)
    for k in range(n_y):
        pre, back = now
        if k + 1 < n_y:
            now = dots(k + 1)
        cdf = 0.5 * (1.0 + lax.erf(pre * 0.7071067811865476))
        dens = jnp.exp(-0.5 * pre * pre) * 0.3989422804014327
        hidden32 = pre * cdf
        new = (back * (cdf + pre * dens)).astype(BF)
        hid = hidden32.astype(BF)
        for c in range(2):
            dpre[c, :, k * unit : (k + 1) * unit] = new[:, c * unit : (c + 1) * unit]
            hidden[c, :, k * unit : (k + 1) * unit] = hid[:, c * unit : (c + 1) * unit]
        by_row = hidden32 * back
        term = by_row if k == 0 else term + by_row
        if k > 0:
            part = dot(grad, w_in_of(k - 1), NN)
            total = part if k == 1 else total + part
        grad = new
    total = total + dot(grad, w_in_of(n_y - 1), NN)
    line = jnp.sum(term.T, axis=0, keepdims=True)
    at = 0
    for (count, is_own), out in zip(blocks, dxs):
        out[0:count] = total[at : at + count].astype(out.dtype)
        here = line[:, at : at + count]
        if is_own:
            by_bias = (d[at : at + count].astype(F32) * b_out[...].astype(F32)).T
            here = here + jnp.sum(by_bias, axis=0, keepdims=True)
            out[count:] = lines_of([here], width, F32)
        else:
            out[count:] = lines_of(high_low(here), width, BF)
        at += count


def rows_set(xs, ds, blocks, w, b_out):
    width = b_out.shape[1]
    m = sum(count for count, _ in blocks)
    units = 4 * (w[0].shape[0] - EXTRA)
    part = jax.ShapeDtypeStruct((2, m, units // 2), BF)
    dxs = [shape(count + EXTRA, width, F32 if own else BF) for count, own in blocks]
    return call(
        functools.partial(rows_kernel, len(xs), len(ds), blocks),
        "rows",
        [shape(m, width), shape(m, width), part, part, *dxs],
        [*xs, *ds, *w, b_out],
        flops=6 * m * units * width,
        vmem=26,
    )


def keep_kernel(ref, out):
    out[...] = ref[...]


def join_kernel(*refs):
    cap = refs[0].shape[1]
    for k, ref in enumerate(refs[:-1]):
        refs[-1][k * cap : (k + 1) * cap] = ref[0]


def stack_kernel(*refs):
    for k, ref in enumerate(refs[:-1]):
        refs[-1][k] = ref[...]


def sums_kernel(x, d, dpre, hidden, out):
    for c in range(2):
        grads = weight_sums(x[...], d[...], dpre[c], hidden[c])
        at = 0
        for g in grads:
            out[c, at : at + g.shape[0]] = g
            at += g.shape[0]


def weight_sums(x, d, dpre, hidden):
    grad_in = dot(dpre, x, TN)
    grad_out = dot(hidden, d, TN)
    line_in = jnp.sum(dpre.astype(F32), axis=0, keepdims=True)
    line_out = jnp.sum(d.astype(F32), axis=0, keepdims=True)
    line_in = jnp.concatenate(
        [line_in, jnp.zeros((1, d.shape[1] - dpre.shape[1]), F32)], axis=1
    )
    return grad_in, grad_out, lines_of([line_in, line_out], d.shape[1], F32)


def away_kernel(near, x, d, dpre, hidden, out):
    grad_in, grad_out, lines = weight_sums(x[...], d[...], dpre[0], hidden[0])
    units = grad_in.shape[0]
    out[0:units] = (near[0, 0:units] + grad_in).astype(BF)
    out[units : 2 * units] = (near[0, units : 2 * units] + grad_out).astype(BF)
    lines = near[0, 2 * units :] + lines
    out[2 * units :] = lines_of(high_low(lines[0:1]) + high_low(lines[1:2]), out.shape[1], BF)


def home_kernel(near, x, d, dpre, hidden, out):
    at = 0
    for g in weight_sums(x[...], d[...], dpre[0], hidden[0]):
        rows = slice(at, at + g.shape[0])
        out[rows] = near[0, rows] + g
        at += g.shape[0]


def merge_kernel(own, got, *outs):
    units = (own.shape[0] - EXTRA) // 2
    width = own.shape[1]
    lines = own[2 * units : 2 * units + 2]
    side = got[2 * units : 2 * units + 4].astype(F32)
    sum_out = lines[1:2] + side[2:3] + side[3:4]
    side = side[0:1] + side[1:2]
    n_y = len(outs)
    unit = units // n_y
    for k, out in enumerate(outs):
        here = k * unit
        line = lines[0:1, here : here + unit] + side[:, here : here + unit]
        line = jnp.concatenate([line, jnp.zeros((1, width - unit), F32)], axis=1)
        for at in (0, unit):
            rows = slice(at, at + unit)
            from_ = slice(n_y * at + here, n_y * at + here + unit)
            total = own[from_] + got[from_].astype(F32)
            out[rows] = total.astype(out.dtype)
        if k == 0:
            both = [line, jnp.zeros_like(line), sum_out]
        else:
            both = high_low(line) + high_low(sum_out)
        out[2 * unit :] = lines_of(both, width, out.dtype)


def last_kernel(own, a, b, c, grad_in, grad_bias_in, grad_out, grad_bias_out):
    units = grad_out.shape[1]
    total = own[...] + a[...].astype(F32) + b[...].astype(F32) + c[...].astype(F32)
    grad_in[0] = total[0:units].T.astype(BF)
    grad_out[0] = total[units : 2 * units].astype(BF)
    tail = total[2 * units :]
    grad_bias_in[...] = (tail[0:1] + tail[1:2])[:, 0:units]
    grad_bias_out[...] = tail[2:3] + tail[3:4]


ORDER = (0, 1, 3, 2)


def sum_kernel(n_early, *refs):
    early, late, (far, out) = refs[:3], refs[3:6], refs[6:]
    n_expert = out.shape[0]
    here = lax.axis_index("x")
    width = far.shape[1]
    m = far.shape[0] - EXTRA
    cap = m // n_expert
    e = sum(r[...].astype(F32) for r in early)
    t = sum(r[...].astype(F32) for r in late)
    cut = n_early * cap
    line = [v[n : n + 1, 0:n] + v[n + 1 : n + 2, 0:n] for v, n in ((e, cut), (t, m - cut))]
    side = far[m : m + 2].astype(F32)
    line = jnp.concatenate(line, axis=1) + side[0:1, 0:m] + side[1:2, 0:m]
    lines = lines_of(high_low(line), width, BF)
    for k, s in enumerate(ORDER):
        to = lax.rem(here + (n_expert - s), n_expert)
        rows = slice(k * cap, (k + 1) * cap)
        total = e[rows] if k < n_early else t[k * cap - cut : (k + 1) * cap - cut]
        out[to, 0:cap] = (total + far[rows].astype(F32)).astype(BF)
        out[to, cap:] = lines


def finish_kernel(places, weights, pieces, out, by_weight):
    n_expert = pieces.shape[0]
    cap = pieces.shape[1] - EXTRA
    n_tok = places.shape[1]
    here = lax.axis_index("x")
    total = None
    sums = [None, None]
    spots = lax.broadcasted_iota(jnp.int32, (n_expert * cap, n_tok), 0)
    picks = [jnp.where(places[k : k + 1, :] == spots, 1.0, 0.0) for k in range(2)]
    both = (picks[0] + picks[1]).astype(BF)
    for s in range(n_expert):
        piece = pieces.at[lax.rem(here + s, n_expert)]
        part = dot(both[s * cap : (s + 1) * cap], piece[0:cap], TN)
        total = part if total is None else total + part
        lane = spots - ORDER.index(s) * cap
        inside = (lane >= 0) & (lane < cap)
        for k in range(2):
            pick = inside & (places[k : k + 1, :] == lane + s * cap)
            pick = jnp.where(pick, 1.0, 0.0).astype(BF)
            found = dot(piece[cap:, 0 : n_expert * cap], pick, NN)
            line = found[0:1] + found[1:2]
            sums[k] = line if sums[k] is None else sums[k] + line
    out[...] = total.astype(BF)
    by_weight[...] = jnp.concatenate(sums, axis=0) / weights[...].astype(F32)


def on_device(tokens, grads_out, routes, slots, combine, w_in, b_in, w_out, b_out):
    n_expert = lax.axis_size("x")
    tok_rows, width = tokens.shape
    cap = 2 * tok_rows // n_expert
    units = w_in.shape[2]

    barrier = lax.optimization_barrier

    mine, raw, places, *x_sent = call_loading(
        prepare_kernel,
        "prepare",
        [
            shape(2 * units + EXTRA, width),
            shape(tok_rows + EXTRA, width),
            shape(2, tok_rows, jnp.int32),
        ]
        + [jax.ShapeDtypeStruct((2, cap, width), BF)] * n_expert,
        [routes.T, slots.T, combine.T, tokens, grads_out, w_in, b_in, w_out],
    )
    raw_below = shift(raw, "z", 1)
    raw_above = shift(raw, "z", -1)
    x_1 = shift(x_sent[1], "x", 1)
    x_3 = shift(x_sent[3], "x", -1)
    w_below = shift(mine, "y", 1)
    w_above = shift(mine, "y", -1)
    x_0 = call(keep_kernel, "keep", [jax.ShapeDtypeStruct((2, cap, width), BF)], [x_sent[0]])[0]
    raw_below, raw_above, x_0, x_1, x_2, x_3 = barrier(
        (raw_below, raw_above, x_0, x_1, x_sent[2], x_3)
    )
    raw_far = shift(raw_below, "z", 1)
    x_2 = shift(x_2, "x", 2)
    x_got = [x_0, x_1, x_3, x_2]
    x_own = call(join_kernel, "join", [shape(n_expert * cap, width)], x_got)[0]
    x_own, raw_far, w_below, w_above = barrier((x_own, raw_far, w_below, w_above))

    d_sent = call(
        douts_kernel,
        "douts",
        [jax.ShapeDtypeStruct((3, cap, width), BF)] * n_expert,
        [raw_below, raw_above, raw_far],
    )
    x_below = shift(x_own, "z", 1)
    x_above = shift(x_own, "z", -1)
    w_far = shift(w_below, "y", 1)
    d_1 = shift(d_sent[1], "x", 1)
    d_3 = shift(d_sent[3], "x", -1)
    x_below, x_above, w_far, d_1, d_3, d_2 = barrier(
        (x_below, x_above, w_far, d_1, d_3, d_sent[2])
    )
    ours = [mine, w_below, w_above, w_far]
    every = call(stack_kernel, "stack", [jax.ShapeDtypeStruct((4, *mine.shape), BF)], ours, vmem=12)
    w = [*ours, shift(every[0], "c", 1)]

    d_2 = shift(d_2, "x", 2)
    half = x_own.shape[0] // 2
    x_far_a = shift(x_below[:half], "z", 1)
    x_far_b = shift(x_above[half:], "z", -1)
    n_early = 3
    cut = n_early * cap
    sides = (x_own, x_below, x_above)
    early = rows_set(
        [(a, 0, cut) for a in sides],
        [(a, 1) for a in x_got[:3]] + [(a, z) for z in range(2) for a in (d_sent[0], d_1, d_3)],
        [(cut, True), (cut, False), (cut, False)],
        w,
        b_out,
    )
    acc = call(
        sums_kernel,
        "sums",
        [jax.ShapeDtypeStruct((2, 8 * units + EXTRA, width), F32)],
        early[:4],
        flops=8 * 3 * cut * 4 * units * width,
        vmem=28,
    )[0]
    early_above = shift(early[6], "z", 1)
    early_below = shift(early[5], "z", -1)
    d_2, x_far_a, x_far_b, acc = barrier((d_2, x_far_a, x_far_b, acc))
    late = rows_set(
        [(a, cut, cap) for a in sides] + [x_far_a, x_far_b],
        [(x_2, 1), (d_2, 0), (d_2, 1)] + [(a, 2) for a in (d_sent[0], d_1, d_3, d_2)],
        [(cap, True), (cap, False), (cap, False), (n_expert * cap, False)],
        w,
        b_out,
    )

    ends = [late[0], late[1], late[2], late[3]]
    flops = 4 * 7 * cap * 4 * units * width
    out = shape(8 * units + EXTRA, width)
    operands = [(acc, 1), *ends[:2], (late[2], 1), (late[3], 1)]
    away = call(away_kernel, "away", [out], operands, flops, vmem=20)[0]
    away, early_above, early_below = barrier((away, early_above, early_below))
    got = shift(away, "c", 1)
    out = shape(8 * units + EXTRA, width, F32)
    operands = [(acc, 0), *ends[:2], (late[2], 0), (late[3], 0)]
    home = call(home_kernel, "home", [out], operands, flops, vmem=24)[0]
    home = call(
        merge_kernel,
        "merge",
        [shape(2 * units + EXTRA, width, BF if k else F32) for k in range(4)],
        [home, got],
        vmem=16,
    )

    far = shift(late[7], "z", 2)
    late_above = shift(late[6], "z", 1)
    late_below = shift(late[5], "z", -1)
    pieces = call(
        functools.partial(sum_kernel, n_early),
        "sum_z",
        [jax.ShapeDtypeStruct((n_expert, cap + EXTRA, width), BF)],
        [early[4], early_above, early_below, late[4], late_above, late_below, far],
    )[0]
    final = lax.all_to_all(pieces, "x", 0, 0, tiled=True)
    moved = [shift(home[k], "y", step) for k, step in ((3, 2), (1, -1), (2, 1))]
    grad_tokens, by_weight = call(
        finish_kernel,
        "finish",
        [shape(tok_rows, width), shape(2, tok_rows, F32)],
        [places, combine.T, final],
    )
    grad_w_in, grad_b_in, grad_w_out, grad_b_out = call(
        last_kernel,
        "last",
        [
            jax.ShapeDtypeStruct(w_in.shape, BF),
            shape(1, units, F32),
            jax.ShapeDtypeStruct(w_out.shape, BF),
            shape(1, width, F32),
        ],
        [home[0], *moved],
    )
    return (grad_tokens, by_weight.T, grad_w_in, grad_b_in, grad_w_out, grad_b_out)


def solution(mesh):
    fine = Mesh(mesh.devices.reshape(4, 4, 4, 2), ("x", "z", "y", "c"))
    zero = ("z", "y", "c")
    rows = P(("x", "z", "y", "c"), None)
    in_specs = (rows,) * 5 + (
        P("x", None, zero),
        P("x", zero),
        P("x", zero, None),
        P("x", None),
    )
    out_specs = (rows, rows) + in_specs[5:]
    return jax.shard_map(
        on_device, mesh=fine, in_specs=in_specs, out_specs=out_specs, check_vma=False
    )
```

```python
import functools

import jax
import jax.numpy as jnp
from jax import lax
from jax.experimental import pallas as pl
from jax.experimental.pallas import tpu as pltpu
from jax.sharding import Mesh, PartitionSpec as P

BF = jnp.bfloat16
F32 = jnp.float32
EXTRA = 16
NT = (((1,), (1,)), ((), ()))
NN = (((1,), (0,)), ((), ()))
TN = (((0,), (0,)), ((), ()))


def dot(a, b, dims):
    return lax.dot_general(a, b, dims, preferred_element_type=F32)


def shift(value, axis, step):
    n = lax.axis_size(axis)
    return lax.ppermute(value, axis, [(i, (i + step) % n) for i in range(n)])


def shape(rows, columns, dtype=BF):
    return jax.ShapeDtypeStruct((rows, columns), dtype)


def full(a):
    return pl.BlockSpec(a.shape, lambda i: (0,) * len(a.shape))


def span(a, first, rows):
    return pl.BlockSpec((rows, a.shape[1]), lambda i: (first // rows, 0))


def lead(a, index):
    return pl.BlockSpec((1, *a.shape[1:]), lambda i: (index,) + (0,) * (len(a.shape) - 1))


def call(kernel, name, out_shape, operands, flops=0, scratch=(), vmem=8):
    parts = [o if isinstance(o, tuple) else (o,) for o in operands]
    size = sum(p[0].size * p[0].dtype.itemsize for p in parts)
    size += sum(s.size * s.dtype.itemsize for s in out_shape)
    return pl.pallas_call(
        kernel,
        out_shape=out_shape,
        grid=(1,),
        in_specs=[(full, lead, span)[len(p) - 1](*p) for p in parts],
        out_specs=[full(s) for s in out_shape],
        scratch_shapes=scratch,
        compiler_params=pltpu.CompilerParams(vmem_limit_bytes=vmem * 1024 * 1024),
        cost_estimate=pl.CostEstimate(flops=flops, bytes_accessed=size, transcendentals=0),
        name=name,
    )(*[p[0] for p in parts])


def call_loading(kernel, name, out_shape, arrays):
    n = len(arrays)

    def body(*refs):
        sources, outs = refs[:n], refs[n : n + len(out_shape)]
        copies, sems = refs[n + len(out_shape) : -1], refs[-1]
        moves = [
            pltpu.make_async_copy(a, b, sems.at[k])
            for k, (a, b) in enumerate(zip(sources, copies))
        ]
        for m in moves:
            m.start()
        for m in moves:
            m.wait()
        kernel(*copies, *outs)

    return pl.pallas_call(
        body,
        out_shape=out_shape,
        in_specs=[pl.BlockSpec(memory_space=pl.ANY)] * n,
        out_specs=[pl.BlockSpec(memory_space=pltpu.VMEM)] * len(out_shape),
        scratch_shapes=[pltpu.VMEM(a.shape, a.dtype) for a in arrays]
        + [pltpu.SemaphoreType.DMA((n,))],
        compiler_params=pltpu.CompilerParams(vmem_limit_bytes=56 * 1024 * 1024),
        name=name,
    )(*arrays)


def high_low(value):
    high = value.astype(BF).astype(F32)
    return [high, value - high]


def lines_of(lines, width, dtype):
    m = lines[0].shape[1]
    rest = EXTRA - sum(line.shape[0] for line in lines)
    block = jnp.concatenate(lines + [jnp.zeros((rest, m), F32)], axis=0)
    if m < width:
        block = jnp.concatenate([block, jnp.zeros((EXTRA, width - m), F32)], axis=1)
    return block.astype(dtype)


def prepare_kernel(
    routes, slots, combine, tokens, grads, w_in, b_in, w_out, share, raw, places, *outs
):
    units = w_out.shape[1]
    share[0:units] = w_in[0].astype(F32).T.astype(BF)
    share[units : units + EXTRA] = lines_of([b_in[...].astype(F32)], share.shape[1], BF)
    share[units + EXTRA :] = w_out[0]
    n_expert = len(outs)
    cap = outs[0].shape[1]
    n_tok = tokens.shape[0]
    turned = routes[...] - lax.axis_index("x")
    turned = jnp.where(turned < 0, turned + n_expert, turned)
    place = jnp.where(slots[...] < cap, turned * cap + slots[...], -1)
    places[...] = place
    raw[0:n_tok] = grads[...]
    side = [place.astype(F32), combine[...].astype(F32)]
    raw[n_tok:] = lines_of(side, grads.shape[1], BF)
    spots = lax.broadcasted_iota(jnp.int32, (n_expert * cap, n_tok), 0)
    first, second = place[0:1] == spots, place[1:2] == spots
    picks = jnp.where(first | second, 1.0, 0.0)
    weights = combine[...].astype(F32)
    scaled = jnp.where(first, weights[0:1], 0.0) + jnp.where(second, weights[1:2], 0.0)
    rows_x = dot(picks.astype(BF), tokens[...], NN).astype(BF)
    rows_d = dot(scaled.astype(BF), grads[...], NN).astype(BF)
    for s, out in enumerate(outs):
        out[0] = rows_x[s * cap : (s + 1) * cap]
        out[1] = rows_d[s * cap : (s + 1) * cap]


def douts_kernel(below, above, far, *outs):
    cap = outs[0].shape[1]
    n_tok = below.shape[0] - EXTRA
    for z, raw in enumerate((below[...], above[...], far[...])):
        side = raw[n_tok : n_tok + 4, 0:n_tok].astype(F32)
        spots = lax.broadcasted_iota(jnp.int32, (len(outs) * cap, n_tok), 0)
        place = side[0:2].astype(jnp.int32)
        picks = jnp.where(place[0:1] == spots, side[2:3], 0.0)
        picks = picks + jnp.where(place[1:2] == spots, side[3:4], 0.0)
        rows = dot(picks.astype(BF), raw[0:n_tok], NN).astype(BF)
        for s, out in enumerate(outs):
            out[z] = rows[s * cap : (s + 1) * cap]


def rows_kernel(n_x, n_d, blocks, *refs):
    xs, ds = refs[:n_x], refs[n_x : n_x + n_d]
    mine, below, above, far, other, others, b_out, *outs = refs[n_x + n_d :]
    x, d, dpre, hidden, *dxs = outs
    shares = [(mine, other)]
    shares += [(ours, others.at[k]) for k, ours in enumerate((below, above, far))]
    width = x.shape[1]
    for parts, whole in ((xs, x), (ds, d)):
        at = 0
        for p in parts:
            count = p.shape[-2]
            whole[at : at + count] = p[...].reshape(count, width)
            at += count
    n_y = len(shares)
    unit = (mine.shape[0] - EXTRA) // 2
    xb = x[...]
    db = d[...]

    def w_in_of(k):
        return jnp.concatenate([r[0:unit] for r in shares[k]], axis=0)

    def dots(k):
        bias = jnp.concatenate([r[unit : unit + 1, 0:unit] for r in shares[k]], axis=1)
        w_out = jnp.concatenate([r[unit + EXTRA :] for r in shares[k]], axis=0)
        return dot(xb, w_in_of(k), NT) + bias.astype(F32), dot(db, w_out, NT)

    term = total = grad = None
    now = dots(0)
    for k in range(n_y):
        pre, back = now
        if k + 1 < n_y:
            now = dots(k + 1)
        cdf = 0.5 * (1.0 + lax.erf(pre * 0.7071067811865476))
        dens = jnp.exp(-0.5 * pre * pre) * 0.3989422804014327
        hidden32 = pre * cdf
        new = (back * (cdf + pre * dens)).astype(BF)
        hid = hidden32.astype(BF)
        for c in range(2):
            dpre[c, :, k * unit : (k + 1) * unit] = new[:, c * unit : (c + 1) * unit]
            hidden[c, :, k * unit : (k + 1) * unit] = hid[:, c * unit : (c + 1) * unit]
        by_row = hidden32 * back
        term = by_row if k == 0 else term + by_row
        if k > 0:
            part = dot(grad, w_in_of(k - 1), NN)
            total = part if k == 1 else total + part
        grad = new
    total = total + dot(grad, w_in_of(n_y - 1), NN)
    line = jnp.sum(term.T, axis=0, keepdims=True)
    at = 0
    for (count, is_own), out in zip(blocks, dxs):
        out[0:count] = total[at : at + count].astype(out.dtype)
        here = line[:, at : at + count]
        if is_own:
            by_bias = (d[at : at + count].astype(F32) * b_out[...].astype(F32)).T
            here = here + jnp.sum(by_bias, axis=0, keepdims=True)
            out[count:] = lines_of([here], width, F32)
        else:
            out[count:] = lines_of(high_low(here), width, BF)
        at += count


def rows_set(xs, ds, blocks, w, b_out):
    width = b_out.shape[1]
    m = sum(count for count, _ in blocks)
    units = 4 * (w[0].shape[0] - EXTRA)
    part = jax.ShapeDtypeStruct((2, m, units // 2), BF)
    dxs = [shape(count + EXTRA, width, F32 if own else BF) for count, own in blocks]
    return call(
        functools.partial(rows_kernel, len(xs), len(ds), blocks),
        "rows",
        [shape(m, width), shape(m, width), part, part, *dxs],
        [*xs, *ds, *w, b_out],
        flops=6 * m * units * width,
        vmem=26,
    )


def join_kernel(*refs):
    cap = refs[0].shape[1]
    for k, ref in enumerate(refs[:-1]):
        refs[-1][k * cap : (k + 1) * cap] = ref[0]


def stack_kernel(*refs):
    for k, ref in enumerate(refs[:-1]):
        refs[-1][k] = ref[...]


def sums_kernel(x, d, dpre, hidden, out):
    for c in range(2):
        grads = weight_sums(x[...], d[...], dpre[c], hidden[c])
        at = 0
        for g in grads:
            out[c, at : at + g.shape[0]] = g
            at += g.shape[0]


def weight_sums(x, d, dpre, hidden):
    grad_in = dot(dpre, x, TN)
    grad_out = dot(hidden, d, TN)
    line_in = jnp.sum(dpre.astype(F32), axis=0, keepdims=True)
    line_out = jnp.sum(d.astype(F32), axis=0, keepdims=True)
    line_in = jnp.concatenate(
        [line_in, jnp.zeros((1, d.shape[1] - dpre.shape[1]), F32)], axis=1
    )
    return grad_in, grad_out, lines_of([line_in, line_out], d.shape[1], F32)


def away_kernel(near, x, d, dpre, hidden, out):
    grad_in, grad_out, lines = weight_sums(x[...], d[...], dpre[0], hidden[0])
    units = grad_in.shape[0]
    out[0:units] = (near[0, 0:units] + grad_in).astype(BF)
    out[units : 2 * units] = (near[0, units : 2 * units] + grad_out).astype(BF)
    lines = near[0, 2 * units :] + lines
    out[2 * units :] = lines_of(high_low(lines[0:1]) + high_low(lines[1:2]), out.shape[1], BF)


def home_kernel(near, x, d, dpre, hidden, out):
    at = 0
    for g in weight_sums(x[...], d[...], dpre[0], hidden[0]):
        rows = slice(at, at + g.shape[0])
        out[rows] = near[0, rows] + g
        at += g.shape[0]


def merge_kernel(own, got, *outs):
    units = (own.shape[0] - EXTRA) // 2
    width = own.shape[1]
    lines = own[2 * units : 2 * units + 2]
    side = got[2 * units : 2 * units + 4].astype(F32)
    sum_out = lines[1:2] + side[2:3] + side[3:4]
    side = side[0:1] + side[1:2]
    n_y = len(outs)
    unit = units // n_y
    for k, out in enumerate(outs):
        here = k * unit
        line = lines[0:1, here : here + unit] + side[:, here : here + unit]
        line = jnp.concatenate([line, jnp.zeros((1, width - unit), F32)], axis=1)
        for at in (0, unit):
            rows = slice(at, at + unit)
            from_ = slice(n_y * at + here, n_y * at + here + unit)
            total = own[from_] + got[from_].astype(F32)
            out[rows] = total.astype(out.dtype)
        if k == 0:
            both = [line, jnp.zeros_like(line), sum_out]
        else:
            both = high_low(line) + high_low(sum_out)
        out[2 * unit :] = lines_of(both, width, out.dtype)


def last_kernel(own, a, b, c, grad_in, grad_bias_in, grad_out, grad_bias_out):
    units = grad_out.shape[1]
    total = own[...] + a[...].astype(F32) + b[...].astype(F32) + c[...].astype(F32)
    grad_in[0] = total[0:units].T.astype(BF)
    grad_out[0] = total[units : 2 * units].astype(BF)
    tail = total[2 * units :]
    grad_bias_in[...] = (tail[0:1] + tail[1:2])[:, 0:units]
    grad_bias_out[...] = tail[2:3] + tail[3:4]


ORDER = (0, 1, 3, 2)


def sum_kernel(n_early, *refs):
    early, late, (far, out) = refs[:3], refs[3:6], refs[6:]
    n_expert = out.shape[0]
    here = lax.axis_index("x")
    width = far.shape[1]
    m = far.shape[0] - EXTRA
    cap = m // n_expert
    e = sum(r[...].astype(F32) for r in early)
    t = sum(r[...].astype(F32) for r in late)
    cut = n_early * cap
    line = [v[n : n + 1, 0:n] + v[n + 1 : n + 2, 0:n] for v, n in ((e, cut), (t, m - cut))]
    side = far[m : m + 2].astype(F32)
    line = jnp.concatenate(line, axis=1) + side[0:1, 0:m] + side[1:2, 0:m]
    lines = lines_of(high_low(line), width, BF)
    for k, s in enumerate(ORDER):
        to = lax.rem(here + (n_expert - s), n_expert)
        rows = slice(k * cap, (k + 1) * cap)
        total = e[rows] if k < n_early else t[k * cap - cut : (k + 1) * cap - cut]
        out[to, 0:cap] = (total + far[rows].astype(F32)).astype(BF)
        out[to, cap:] = lines


def finish_kernel(places, weights, pieces, out, by_weight):
    n_expert = pieces.shape[0]
    cap = pieces.shape[1] - EXTRA
    n_tok = places.shape[1]
    here = lax.axis_index("x")
    total = None
    sums = [None, None]
    spots = lax.broadcasted_iota(jnp.int32, (n_expert * cap, n_tok), 0)
    picks = [jnp.where(places[k : k + 1, :] == spots, 1.0, 0.0) for k in range(2)]
    both = (picks[0] + picks[1]).astype(BF)
    for s in range(n_expert):
        piece = pieces.at[lax.rem(here + s, n_expert)]
        part = dot(both[s * cap : (s + 1) * cap], piece[0:cap], TN)
        total = part if total is None else total + part
        lane = spots - ORDER.index(s) * cap
        inside = (lane >= 0) & (lane < cap)
        for k in range(2):
            pick = inside & (places[k : k + 1, :] == lane + s * cap)
            pick = jnp.where(pick, 1.0, 0.0).astype(BF)
            found = dot(piece[cap:, 0 : n_expert * cap], pick, NN)
            line = found[0:1] + found[1:2]
            sums[k] = line if sums[k] is None else sums[k] + line
    out[...] = total.astype(BF)
    by_weight[...] = jnp.concatenate(sums, axis=0) / weights[...].astype(F32)


def on_device(tokens, grads_out, routes, slots, combine, w_in, b_in, w_out, b_out):
    n_expert = lax.axis_size("x")
    tok_rows, width = tokens.shape
    cap = 2 * tok_rows // n_expert
    units = w_in.shape[2]

    barrier = lax.optimization_barrier

    mine, raw, places, *x_sent = call_loading(
        prepare_kernel,
        "prepare",
        [
            shape(2 * units + EXTRA, width),
            shape(tok_rows + EXTRA, width),
            shape(2, tok_rows, jnp.int32),
        ]
        + [jax.ShapeDtypeStruct((2, cap, width), BF)] * n_expert,
        [routes.T, slots.T, combine.T, tokens, grads_out, w_in, b_in, w_out],
    )
    raw_below = shift(raw, "z", 1)
    raw_above = shift(raw, "z", -1)
    x_1 = shift(x_sent[1], "x", 1)
    x_3 = shift(x_sent[3], "x", -1)
    w_below = shift(mine, "y", 1)
    w_above = shift(mine, "y", -1)
    raw_below, raw_above, x_1, x_2, x_3 = barrier((raw_below, raw_above, x_1, x_sent[2], x_3))
    raw_far = shift(raw_below, "z", 1)
    x_2 = shift(x_2, "x", 2)
    x_got = [x_sent[0], x_1, x_3, x_2]
    x_own = call(join_kernel, "join", [shape(n_expert * cap, width)], x_got)[0]
    other = shift(mine, "c", 1)
    x_own, raw_far, w_below, w_above, other = barrier((x_own, raw_far, w_below, w_above, other))

    d_sent = call(
        douts_kernel,
        "douts",
        [jax.ShapeDtypeStruct((3, cap, width), BF)] * n_expert,
        [raw_below, raw_above, raw_far],
    )
    x_below = shift(x_own, "z", 1)
    x_above = shift(x_own, "z", -1)
    w_far = shift(w_below, "y", 1)
    d_1 = shift(d_sent[1], "x", 1)
    d_3 = shift(d_sent[3], "x", -1)
    x_below, x_above, w_far, d_1, d_3, d_2 = barrier(
        (x_below, x_above, w_far, d_1, d_3, d_sent[2])
    )
    ours = [mine, w_below, w_above, w_far]
    rest = [jax.ShapeDtypeStruct((3, *mine.shape), BF)]
    rest = call(stack_kernel, "stack", rest, ours[1:], vmem=12)[0]
    w = [*ours, other, shift(rest, "c", 1)]

    d_2 = shift(d_2, "x", 2)
    half = x_own.shape[0] // 2
    x_far_a = shift(x_below[:half], "z", 1)
    x_far_b = shift(x_above[half:], "z", -1)
    n_early = 3
    cut = n_early * cap
    sides = (x_own, x_below, x_above)
    early = rows_set(
        [(a, 0, cut) for a in sides],
        [(a, 1) for a in x_got[:3]] + [(a, z) for z in range(2) for a in (d_sent[0], d_1, d_3)],
        [(cut, True), (cut, False), (cut, False)],
        w,
        b_out,
    )
    acc = call(
        sums_kernel,
        "sums",
        [jax.ShapeDtypeStruct((2, 8 * units + EXTRA, width), F32)],
        early[:4],
        flops=8 * 3 * cut * 4 * units * width,
        vmem=28,
    )[0]
    early_above = shift(early[6], "z", 1)
    early_below = shift(early[5], "z", -1)
    d_2, x_far_a, x_far_b, acc = barrier((d_2, x_far_a, x_far_b, acc))
    late = rows_set(
        [(a, cut, cap) for a in sides] + [x_far_a, x_far_b],
        [(x_2, 1), (d_2, 0), (d_2, 1)] + [(a, 2) for a in (d_sent[0], d_1, d_3, d_2)],
        [(cap, True), (cap, False), (cap, False), (n_expert * cap, False)],
        w,
        b_out,
    )

    ends = [late[0], late[1], late[2], late[3]]
    flops = 4 * 7 * cap * 4 * units * width
    out = shape(8 * units + EXTRA, width)
    operands = [(acc, 1), *ends[:2], (late[2], 1), (late[3], 1)]
    away = call(away_kernel, "away", [out], operands, flops, vmem=20)[0]
    away, early_above, early_below = barrier((away, early_above, early_below))
    got = shift(away, "c", 1)
    out = shape(8 * units + EXTRA, width, F32)
    operands = [(acc, 0), *ends[:2], (late[2], 0), (late[3], 0)]
    home = call(home_kernel, "home", [out], operands, flops, vmem=24)[0]
    home = call(
        merge_kernel,
        "merge",
        [shape(2 * units + EXTRA, width, BF if k else F32) for k in range(4)],
        [home, got],
        vmem=16,
    )

    far = shift(late[7], "z", 2)
    late_above = shift(late[6], "z", 1)
    late_below = shift(late[5], "z", -1)
    pieces = call(
        functools.partial(sum_kernel, n_early),
        "sum_z",
        [jax.ShapeDtypeStruct((n_expert, cap + EXTRA, width), BF)],
        [early[4], early_above, early_below, late[4], late_above, late_below, far],
    )[0]
    final = lax.all_to_all(pieces, "x", 0, 0, tiled=True)
    moved = [shift(home[k], "y", step) for k, step in ((3, 2), (1, -1), (2, 1))]
    grad_tokens, by_weight = call(
        finish_kernel,
        "finish",
        [shape(tok_rows, width), shape(2, tok_rows, F32)],
        [places, combine.T, final],
    )
    grad_w_in, grad_b_in, grad_w_out, grad_b_out = call(
        last_kernel,
        "last",
        [
            jax.ShapeDtypeStruct(w_in.shape, BF),
            shape(1, units, F32),
            jax.ShapeDtypeStruct(w_out.shape, BF),
            shape(1, width, F32),
        ],
        [home[0], *moved],
    )
    return (grad_tokens, by_weight.T, grad_w_in, grad_b_in, grad_w_out, grad_b_out)


def solution(mesh):
    fine = Mesh(mesh.devices.reshape(4, 4, 4, 2), ("x", "z", "y", "c"))
    zero = ("z", "y", "c")
    rows = P(("x", "z", "y", "c"), None)
    in_specs = (rows,) * 5 + (
        P("x", None, zero),
        P("x", zero),
        P("x", zero, None),
        P("x", None),
    )
    out_specs = (rows, rows) + in_specs[5:]
    return jax.shard_map(
        on_device, mesh=fine, in_specs=in_specs, out_specs=out_specs, check_vma=False
    )
```
